256 devices in a mesh: pipe: 2 (over y_lo), dp: 16 (over z, y_hi), tensor: 8 (over x, core).
Axes of the slice: x: 4, y: 4 (y_hi: 2, y_lo: 2; y = y_hi * 2 + y_lo), z: 8, core: 2. Of those that a mesh axis runs over, the one named last changes fastest.
Arguments:
- handoff: bfloat16 [2, 32768, 1024], P('pipe', 'dp', 'tensor'), may hold values from -6 to 6
- hidden_pre: bfloat16 [2, 32768, 4096], P('pipe', 'dp', 'tensor'), may hold values from -6 to 6
- down_weight: bfloat16 [2, 4096, 1024], P('pipe', 'tensor'), may hold values from -6 to 6
- up_weight: bfloat16 [2, 4096, 1024], P('pipe', 'tensor'), may hold values from -6 to 6
- moment: float32 [2, 4096, 1024], P('pipe', ('tensor', 'dp')), may hold values from -3 to 3
- second: float32 [2, 4096, 1024], P('pipe', ('tensor', 'dp')), may hold values from 0.05 to 2
Outputs:
- input_grad: bfloat16 [2, 32768, 1024], P('pipe', 'dp', 'tensor')
- new_down: bfloat16 [2, 4096, 1024], P('pipe', 'tensor')
- new_moment: float32 [2, 4096, 1024], P('pipe', ('tensor', 'dp'))
- new_second: float32 [2, 4096, 1024], P('pipe', ('tensor', 'dp'))
The draws below stay inside these ranges and needn't reach their ends.
All inputs are finite; a program needn't handle non-finite values.
Results may differ from the reference program's by a relative error of at most 0.017.
Values may be sent and summed in bfloat16 or wider, within the bound.
A program may use at most 64 MiB of HBM per device.

```python
import math
import jax
import jax.numpy as jnp
from jax import lax

D = 1024
FF = 4096
TOK = 2048
PIPES = 2
HW = 512
TOKENS = 32768
N_DP = 16
N_TENSOR = 8


def with_spikes(array, own_key, source, target, parts, factor):
    def block_of(position):
        return (jnp.arange(array.shape[position]) // (array.shape[position] // parts)).reshape((-1,) + (1,) * (array.ndim - 1 - position))

    first = jax.random.permutation(own_key, parts)[block_of(target)]
    second = (block_of(target) + parts // 2) % parts
    return jnp.where((block_of(source) == first) | (block_of(source) == second), factor * array, array)


def level_of(own_key, dims, cuts, smallest, high):
    def one(dim, blocks):
        steps = jax.random.uniform(jax.random.fold_in(jax.random.fold_in(own_key, 6), dim), (blocks,), jnp.float32, smallest / len(cuts), high / len(cuts))
        return jnp.repeat(jnp.exp(steps), dims[dim] // blocks).reshape((-1,) + (1,) * (len(dims) - dim - 1))

    gain = one(*cuts[0])
    for cut in cuts[1:]:
        gain = gain * one(*cut)
    return gain


def bell_draw(own_key, dims, width, reach, shards=(), held_as=jnp.bfloat16):
    entries = jax.random.normal(own_key, dims, jnp.float32) * width
    if len(shards) > 0:
        entries = level_of(own_key, dims, shards, -0.22, 0.18) * entries
    return jnp.clip(entries, min=-reach, max=reach).astype(held_as)


def gaussian_with(stream_key, dims, deviation, bound, cuts, heavy, held_as=jnp.bfloat16):
    entries = deviation * jax.random.normal(stream_key, dims, jnp.float32)
    if cuts:
        entries = entries * level_of(stream_key, dims, cuts, -0.22, 0.18)
    return jnp.clip(with_spikes(entries, jax.random.fold_in(stream_key, 3), *heavy), -bound, bound).astype(held_as)


def setup_inputs(seed: int = 0) -> dict:
    keys = jax.random.split(jax.random.key(seed), 7)
    handoff = bell_draw(keys[0], (PIPES, TOKENS, D), 1.0, 6.0, ((0, 2), (1, 16), (2, 8)))
    hidden_pre = gaussian_with(keys[1], (PIPES, TOKENS, FF), 1.0, 6.0, ((0, 2), (1, 16), (2, 8)), (1, 2, 16, 2.0))
    down_weight = bell_draw(keys[2], (PIPES, FF, D), 1.0, 6.0, ((0, 2), (1, 8)))
    up_weight = bell_draw(keys[3], (PIPES, FF, D), 1.0, 6.0, ((0, 2), (1, 8)))
    moment = bell_draw(keys[4], (PIPES, FF, D), 0.5, 3.0, ((0, 2), (1, 128)), jnp.float32)
    second = jnp.clip(jnp.exp(math.log(2.0) - 3.6888794 * jax.random.uniform(keys[5], (PIPES, FF, D), jnp.float32) ** level_of(keys[5], (PIPES, FF, D), ((0, 2), (1, 128)), -0.2, 0.2)), 0.05, 2.0)
    return {"handoff": handoff, "hidden_pre": hidden_pre, "down_weight": down_weight, "up_weight": up_weight, "moment": moment, "second": second}


def normal_cdf(inputs):
    return 0.5 * (1.0 + jax.scipy.special.erf(inputs * (1.0 / math.sqrt(2.0))))

def gelu_value(inputs):
    return inputs * normal_cdf(inputs)

def gelu_slope(inputs):
    return normal_cdf(inputs) + inputs * jnp.exp(-0.5 * inputs * inputs) * (1.0 / math.sqrt(2.0 * math.pi))

def reference(handoff, hidden_pre, down_weight, up_weight, moment, second):
    grads_out = []
    downs_out = []
    moments_out = []
    seconds_out = []
    for section_index in range(PIPES):
        incoming = handoff[(section_index + 1) % PIPES]
        pre_values = hidden_pre[section_index].astype(jnp.float32)
        hidden = gelu_value(pre_values).astype(jnp.bfloat16)
        down_back = jnp.dot(incoming, down_weight[section_index].T, preferred_element_type=jnp.float32)
        act_grad = (down_back * (1.0 / math.sqrt(D)) * gelu_slope(pre_values)).astype(jnp.bfloat16)
        running = jnp.zeros((TOKENS, D), jnp.float32)
        for tensor_rank in range(N_TENSOR):
            lower = tensor_rank * HW
            partial_value = jnp.dot(act_grad[:, lower:lower + HW], up_weight[section_index][lower:lower + HW], preferred_element_type=jnp.float32)
            partial_value = lax.optimization_barrier((partial_value * (1.0 / math.sqrt(FF))).astype(jnp.bfloat16))
            running = running + partial_value.astype(jnp.float32)
        grads_out.append(running.astype(jnp.bfloat16))

        def add_term(accum, block_index):
            hidden_rows = lax.dynamic_slice_in_dim(hidden, (block_index * TOK).astype(jnp.int32), TOK, 0)
            cotan_rows = lax.dynamic_slice_in_dim(incoming, (block_index * TOK).astype(jnp.int32), TOK, 0)
            block_term = jnp.dot(hidden_rows.T, cotan_rows, preferred_element_type=jnp.float32)
            block_term = lax.optimization_barrier((block_term * (1.0 / math.sqrt(TOKENS))).astype(jnp.bfloat16))
            return (accum + block_term.astype(jnp.float32), None)
        gradient, _ = lax.scan(add_term, jnp.zeros((FF, D), jnp.float32), jnp.arange(N_DP, dtype=jnp.int32))
        new_m = 0.9 * moment[section_index] + 0.1 * gradient
        new_v = 0.95 * second[section_index] + 0.05 * gradient * gradient
        fresh_rows = down_weight[section_index].astype(jnp.float32) - 0.2 * new_m / (jnp.sqrt(new_v) + 1e-08)
        downs_out.append(fresh_rows.astype(jnp.bfloat16))
        moments_out.append(new_m)
        seconds_out.append(new_v)
    return (jnp.stack(grads_out), jnp.stack(downs_out), jnp.stack(moments_out), jnp.stack(seconds_out))
```

```python
import math

import jax
import jax.numpy as jnp
from jax import lax
from jax.experimental import pallas as pl
from jax.experimental.pallas import tpu as pltpu
from jax.sharding import PartitionSpec as P

F32 = jnp.float32
BF16 = jnp.bfloat16

X = 4
Z = 8
D = 1024
HW = 512
TOK = 2048
FF = 4096
TOKENS = 32768
ROWS = 32
PIECES = 4
PIECE = TOK // PIECES
CHUNKS = 8
CHUNK = TOK // CHUNKS
COLS = D // X
HALF = COLS // 2
N_SENDS = 200


def kernel(
    handoff, pre_in, down_in, up_in, moment_in, second_in,
    grad_out, down_out, moment_out, second_out,
    inc, pre, hidden_t, slope, down, up, moment, second,
    part, part_got, two_got, one_send, one_got, grad,
    term, up_got, dn_got, total, total_half, half_got, new_m, new_v, fresh,
    send, recv, local,
):
    p = lax.axis_index("pipe")
    d = lax.axis_index("dp")
    t = lax.axis_index("tensor")
    z, yh = lax.div(d, 2), lax.rem(d, 2)
    x, c = lax.div(t, 2), lax.rem(t, 2)

    def at_x(k):
        return lax.rem(x + (k + X), X)

    def at_z(k):
        return lax.rem(z + (k + Z), Z)

    across = (1 - p, d, t)
    core = (p, d, x * 2 + (1 - c))
    x_up = (p, d, at_x(1) * 2 + c)
    x_dn = (p, d, at_x(-1) * 2 + c)
    z_up = (p, at_z(1) * 2 + yh, t)
    z_dn = (p, at_z(-1) * 2 + yh, t)
    mate = (p, z * 2 + (1 - yh), t)
    partners = (across, core, x_up, x_dn, z_up, z_dn, mate)

    sent = []

    def put(src, dst, device):
        i = len(sent)
        copy = pltpu.make_async_remote_copy(
            src_ref=src, dst_ref=dst, send_sem=send.at[i], recv_sem=recv.at[i],
            device_id=device, device_id_type=pl.DeviceIdType.MESH,
        )
        copy.start()
        sent.append(copy)
        return copy

    stays = []

    def move(src, dst):
        copy = pltpu.make_async_copy(src, dst, local.at[len(stays)])
        copy.start()
        stays.append(copy)
        return copy

    barrier = pltpu.get_barrier_semaphore()
    for device in partners:
        pl.semaphore_signal(barrier, inc=1, device_id=device, device_id_type=pl.DeviceIdType.MESH)
    in_pre = move(pre_in.at[0], pre)
    in_down = move(down_in.at[0], down)
    in_up = move(up_in.at[0], up)
    in_moment = move(moment_in.at[0], moment)
    in_second = move(second_in.at[0], second)
    pl.semaphore_wait(barrier, len(partners))

    def piece(s):
        return pl.ds(s * PIECE, PIECE)

    slot_of = {k: at_x(k) * 2 + c for k in (0, -1, 1, 2)}
    y_got = [put(handoff.at[0, piece(s)], inc.at[t, piece(s)], across) for s in range(PIECES)]
    dn_piece, up_piece, two_piece, core_piece = {}, {}, {}, {}

    def share(k, s):
        block = inc.at[slot_of[k], piece(s)]
        core_piece[k, s] = put(block, block, core)

    def from_y(s):
        y_got[s].wait_recv()
        block = inc.at[slot_of[0], piece(s)]
        up_piece[s] = put(block, block, x_up)
        dn_piece[s] = put(block, block, x_dn)
        share(0, s)

    def from_below(s):
        up_piece[s].wait_recv()
        block = inc.at[slot_of[-1], piece(s)]
        if s % 2 == 0:
            two_piece[s] = put(block, block, x_up)
        share(-1, s)

    def from_above(s):
        dn_piece[s].wait_recv()
        block = inc.at[slot_of[1], piece(s)]
        if s % 2 == 1:
            two_piece[s] = put(block, block, x_dn)
        share(1, s)

    def from_two(s):
        two_piece[s].wait_recv()
        share(2, s)

    GELU = 128

    def gelu(first, last):
        def body(b, carry):
            rows = pl.ds(pl.multiple_of(b * GELU, GELU), GELU)
            a = pre[rows, :].astype(F32)
            cdf = 0.5 * (1.0 + lax.erf(a * (1.0 / math.sqrt(2.0))))
            slope[rows, :] = cdf + a * jnp.exp(-0.5 * a * a) * (1.0 / math.sqrt(2.0 * math.pi))
            hidden_t[:, rows] = (a * cdf).astype(BF16).T
            return carry

        lax.fori_loop(first, last, body, 0)

    up_sum, dn_sum, half_sum = {}, {}, {}

    def z_rows(k):
        return pl.ds(pl.multiple_of(at_z(k) * 2 * ROWS, 2 * ROWS), 2 * ROWS)

    def terms(k):
        for s in range(PIECES):
            core_piece[k, s].wait_recv()
        xa = at_x(k)
        block = jnp.concatenate([inc[xa * 2], inc[xa * 2 + 1]], axis=1)
        product = jnp.dot(hidden_t[...], block, preferred_element_type=F32)
        term[xa] = (product * (1.0 / math.sqrt(TOKENS))).astype(BF16)
        far = z_rows(4)
        lo, hi = pl.ds(0, HALF), pl.ds(HALF, HALF)
        up_sum[k] = put(term.at[xa, far, lo], up_got.at[xa, 0, :, lo], z_up)
        dn_sum[k] = put(term.at[xa, far, hi], dn_got.at[xa, 0, :, hi], z_dn)

    def add_rows(xa, rows, got, step, cols):
        mine = term[xa, rows, cols].astype(F32) + got[xa, step, :, cols].astype(F32)
        term[xa, rows, cols] = mine.astype(BF16)

    def z_step(k, j):
        xa = at_x(k)
        full = pl.ds(0, COLS)
        rows = z_rows(4 - j)
        up_sum[k].wait_recv()
        add_rows(xa, rows, up_got, j - 1, pl.ds(0, HALF) if j == 1 else full)
        up_sum[k] = put(term.at[xa, rows], up_got.at[xa, j], z_up)
        rows = z_rows(j - 4)
        dn_sum[k].wait_recv()
        add_rows(xa, rows, dn_got, j - 1, pl.ds(HALF, HALF) if j == 1 else full)
        dn_sum[k] = put(term.at[xa, rows], dn_got.at[xa, j], z_dn)

    def z_last(k):
        xa = at_x(k)
        up_sum[k].wait_recv()
        dn_sum[k].wait_recv()
        both = term[xa, z_rows(0)].astype(F32) + up_got[xa, 3].astype(F32) + dn_got[xa, 3].astype(F32)
        total[xa] = both
        total_half[xa] = both.astype(BF16)
        other = pl.ds(pl.multiple_of((1 - yh) * ROWS, ROWS), ROWS)
        half_sum[k] = put(total_half.at[xa, other], half_got.at[xa], mate)

    own_rows = pl.ds(pl.multiple_of(d * ROWS, ROWS), ROWS)

    def adam(k):
        xa = at_x(k)
        cols = pl.ds(pl.multiple_of(xa * COLS, COLS), COLS)
        half_sum[k].wait_recv()
        mine = pl.ds(pl.multiple_of(yh * ROWS, ROWS), ROWS)
        gradient = total[xa, mine] + half_got[xa].astype(F32)
        m = 0.9 * moment[:, cols] + 0.1 * gradient
        v = 0.95 * second[:, cols] + 0.05 * gradient * gradient
        new_m[:, cols] = m
        new_v[:, cols] = v
        old = down[own_rows, cols].astype(F32)
        fresh[own_rows, cols] = (old - 0.2 * m / (jnp.sqrt(v) + 1e-08)).astype(BF16)

    ring_up, ring_dn, side = {}, {}, {}

    def new_rows(k, h, first=0, count=ROWS):
        start = (at_z(k) * 2 + h) * ROWS + first
        return fresh.at[pl.ds(pl.multiple_of(start, count), count)]

    def spread(h, key):
        block = new_rows(0, h)
        ring_up[key] = put(block, block, z_up)
        ring_dn[key] = put(block, block, z_dn)

    def relay(h, key, j):
        part_rows = (0, ROWS) if j < 3 else (0, ROWS // 2)
        ring_up[key].wait_recv()
        block = new_rows(-j, h, *part_rows)
        ring_up[key] = put(block, block, z_up)
        part_rows = (0, ROWS) if j < 3 else (ROWS // 2, ROWS // 2)
        ring_dn[key].wait_recv()
        block = new_rows(j, h, *part_rows)
        ring_dn[key] = put(block, block, z_dn)

    pair, two, one_up, one_dn = {}, {}, {}, {}

    def chunk(i):
        return pl.ds(i * CHUNK, CHUNK)

    def partial(i):
        rows = chunk(i)
        block = jnp.concatenate([inc[s, rows] for s in range(2 * X)], axis=1)
        back = lax.dot_general(block, down[...], (((1,), (1,)), ((), ())), preferred_element_type=F32)
        act = (back * (1.0 / math.sqrt(D)) * slope[rows, :]).astype(BF16)
        value = jnp.dot(act, up[...], preferred_element_type=F32) * (1.0 / math.sqrt(FF))
        value = value.astype(BF16)
        for xa in range(X):
            for ca in range(2):
                s = xa * 2 + ca
                part[ca, xa, rows] = value[:, s * 128 : (s + 1) * 128]
        pair[i] = put(part.at[1 - c, :, rows], part_got.at[:, rows], core)

    def summed(i, k):
        xa = at_x(k)
        rows = chunk(i)
        return part[c, xa, rows].astype(F32) + part_got[xa, rows].astype(F32)

    def x_first(i):
        rows = chunk(i)
        pair[i].wait_recv()
        far, far_dev, near, near_k = (x_up, 0, x_dn, -1) if i % 2 == 0 else (x_dn, 1, x_up, 1)
        one_send[2, rows] = summed(i, 2).astype(BF16)
        two[i] = put(one_send.at[2, rows], two_got.at[rows], far)
        side_n = 1 - far_dev
        one_send[side_n, rows] = summed(i, near_k).astype(BF16)
        one_dn[i] = put(one_send.at[side_n, rows], one_got.at[side_n, rows], near)

    def x_second(i):
        rows = chunk(i)
        far, side_f, k = (x_up, 0, 1) if i % 2 == 0 else (x_dn, 1, -1)
        two[i].wait_recv()
        one_send[side_f, rows] = (summed(i, k) + two_got[rows].astype(F32)).astype(BF16)
        one_up[i] = put(one_send.at[side_f, rows], one_got.at[side_f, rows], far)

    def x_last(i):
        rows = chunk(i)
        one_dn[i].wait_recv()
        one_up[i].wait_recv()
        both = one_got[0, rows].astype(F32) + one_got[1, rows].astype(F32)
        grad[rows] = (summed(i, 0) + both).astype(BF16)

    in_pre.wait()
    gelu(0, 4)
    from_y(0)
    gelu(4, 8)
    from_y(1)
    from_below(0)
    from_above(0)
    gelu(8, 12)
    from_y(2)
    from_below(1)
    from_above(1)
    gelu(12, 16)
    from_y(3)
    from_below(2)
    from_above(2)
    terms(0)
    from_below(3)
    from_above(3)
    z_step(0, 1)
    terms(-1)
    terms(1)
    z_step(0, 2)
    for s in range(PIECES):
        from_two(s)
    z_step(-1, 1)
    z_step(1, 1)
    z_step(0, 3)
    terms(2)
    z_step(-1, 2)
    z_step(1, 2)
    in_down.wait()
    in_up.wait()
    in_moment.wait()
    in_second.wait()
    partial(0)
    z_last(0)
    z_step(2, 1)
    z_step(-1, 3)
    z_step(1, 3)
    partial(1)
    x_first(0)
    z_step(2, 2)
    z_last(-1)
    z_last(1)
    partial(2)
    x_first(1)
    x_second(0)
    z_step(2, 3)
    adam(0)
    adam(-1)
    adam(1)
    partial(3)
    x_first(2)
    x_second(1)
    x_last(0)
    z_last(2)
    partial(4)
    x_first(3)
    x_second(2)
    adam(2)
    spread(yh, "own")
    side = put(new_rows(0, yh), new_rows(0, yh), mate)
    move(new_m, moment_out.at[0])
    move(new_v, second_out.at[0])
    partial(5)
    x_first(4)
    x_second(3)
    x_last(1)
    side.wait_recv()
    spread(1 - yh, "mate")
    partial(6)
    x_first(5)
    x_second(4)
    relay(yh, "own", 1)
    partial(7)
    x_first(6)
    x_second(5)
    relay(1 - yh, "mate", 1)
    x_first(7)
    x_second(6)
    relay(yh, "own", 2)
    x_second(7)
    relay(1 - yh, "mate", 2)
    x_last(2)
    x_last(3)
    x_last(4)
    relay(yh, "own", 3)
    x_last(5)
    relay(1 - yh, "mate", 3)
    x_last(6)
    x_last(7)
    move(grad, grad_out.at[0])
    for key in ("own", "mate"):
        ring_up[key].wait_recv()
        ring_dn[key].wait_recv()
    move(fresh, down_out.at[0])
    for copy in sent:
        copy.wait_send()
    for copy in stays[5:]:
        copy.wait()


def on_device(handoff, hidden_pre, down_weight, up_weight, moment, second):
    anywhere = pl.BlockSpec(memory_space=pl.ANY)
    return pl.pallas_call(
        kernel,
        out_shape=(
            jax.ShapeDtypeStruct((1, TOK, 128), BF16),
            jax.ShapeDtypeStruct((1, HW, D), BF16),
            jax.ShapeDtypeStruct((1, ROWS, D), F32),
            jax.ShapeDtypeStruct((1, ROWS, D), F32),
        ),
        in_specs=[anywhere] * 6,
        out_specs=(anywhere,) * 4,
        scratch_shapes=[
            pltpu.VMEM((2 * X, TOK, 128), BF16),
            pltpu.VMEM((TOK, HW), BF16),
            pltpu.VMEM((HW, TOK), BF16),
            pltpu.VMEM((TOK, HW), F32),
            pltpu.VMEM((HW, D), BF16),
            pltpu.VMEM((HW, D), BF16),
            pltpu.VMEM((ROWS, D), F32),
            pltpu.VMEM((ROWS, D), F32),
            pltpu.VMEM((2, X, TOK, 128), BF16),
            pltpu.VMEM((X, TOK, 128), BF16),
            pltpu.VMEM((TOK, 128), BF16),
            pltpu.VMEM((3, TOK, 128), BF16),
            pltpu.VMEM((2, TOK, 128), BF16),
            pltpu.VMEM((TOK, 128), BF16),
            pltpu.VMEM((X, HW, COLS), BF16),
            pltpu.VMEM((X, 4, 2 * ROWS, COLS), BF16),
            pltpu.VMEM((X, 4, 2 * ROWS, COLS), BF16),
            pltpu.VMEM((X, 2 * ROWS, COLS), F32),
            pltpu.VMEM((X, 2 * ROWS, COLS), BF16),
            pltpu.VMEM((X, ROWS, COLS), BF16),
            pltpu.VMEM((ROWS, D), F32),
            pltpu.VMEM((ROWS, D), F32),
            pltpu.VMEM((HW, D), BF16),
            pltpu.SemaphoreType.DMA((N_SENDS,)),
            pltpu.SemaphoreType.DMA((N_SENDS,)),
            pltpu.SemaphoreType.DMA((16,)),
        ],
        compiler_params=pltpu.CompilerParams(
            collective_id=0, has_side_effects=True, vmem_limit_bytes=56 * 1024 * 1024
        ),
        cost_estimate=pl.CostEstimate(flops=6 * TOK * HW * D, bytes_accessed=12 << 20, transcendentals=2 * TOK * HW),
    )(handoff, hidden_pre, down_weight, up_weight, moment, second)


def solution(mesh):
    placed = (
        P("pipe", "dp", "tensor"),
        P("pipe", "dp", "tensor"),
        P("pipe", "tensor", None),
        P("pipe", "tensor", None),
        P("pipe", ("tensor", "dp"), None),
        P("pipe", ("tensor", "dp"), None),
    )
    return jax.shard_map(
        on_device,
        mesh=mesh,
        in_specs=placed,
        out_specs=(
            P("pipe", "dp", "tensor"),
            P("pipe", "tensor", None),
            P("pipe", ("tensor", "dp"), None),
            P("pipe", ("tensor", "dp"), None),
        ),
        check_vma=False,
    )
```

```python
import math

import jax
import jax.numpy as jnp
from jax import lax
from jax.experimental import pallas as pl
from jax.experimental.pallas import tpu as pltpu
from jax.sharding import PartitionSpec as P

F32 = jnp.float32
BF16 = jnp.bfloat16

X = 4
Z = 8
D = 1024
HW = 512
TOK = 2048
FF = 4096
TOKENS = 32768
ROWS = 32
PIECES = 8
PIECE = TOK // PIECES
CHUNKS = 8
CHUNK = TOK // CHUNKS
COLS = D // X
HALF = COLS // 2


def kernel(
    handoff, pre_in, down_in, up_in, moment_in, second_in,
    grad_out, down_out, moment_out, second_out,
    inc, pre, hidden_t, slope, down, up, moment, second,
    part, part_got, two_got, one_send, one_got, grad,
    term, agg_got, fin_got, so_far, new_m, new_v, fresh,
    y_sem, x_sem, two_sem, core_sem, pair_sem, far_sem, last_sem,
    agg_sem, fin_sem, ring_sem, row_sem, send_sem, local,
):
    p = lax.axis_index("pipe")
    d = lax.axis_index("dp")
    t = lax.axis_index("tensor")
    z, yh = lax.div(d, 2), lax.rem(d, 2)
    x, c = lax.div(t, 2), lax.rem(t, 2)

    def at_x(k):
        return lax.rem(x + (k + X), X)

    def at_z(k):
        return lax.rem(z + (k + Z), Z)

    def at_h(h):
        return 1 - yh if h else yh

    def owner(k, h):
        return (p, at_z(k) * 2 + at_h(h), t)

    across = (1 - p, d, t)
    core = (p, d, x * 2 + (1 - c))
    x_up = (p, d, at_x(1) * 2 + c)
    x_dn = (p, d, at_x(-1) * 2 + c)
    near = [(k, h) for k in (2, -2, 1, -1) for h in (1, 0)]
    partners = (across, core, x_up, x_dn, owner(0, 1)) + tuple(owner(k, h) for k, h in near)

    GATHER, TERMS, NEW, GRAD = range(4)

    def put(src, dst, device, kind, sem):
        pltpu.make_async_remote_copy(
            src_ref=src, dst_ref=dst, send_sem=send_sem.at[kind], recv_sem=sem,
            device_id=device, device_id_type=pl.DeviceIdType.MESH,
        ).start()

    def landed(ref, sem):
        pltpu.make_async_remote_copy(
            src_ref=ref, dst_ref=ref, send_sem=send_sem.at[0], recv_sem=sem,
            device_id=core, device_id_type=pl.DeviceIdType.MESH,
        ).wait_recv()

    def left(ref, kind):
        pltpu.make_async_remote_copy(
            src_ref=ref, dst_ref=ref, send_sem=send_sem.at[kind], recv_sem=row_sem.at[0],
            device_id=core, device_id_type=pl.DeviceIdType.MESH,
        ).wait_send()

    stays = []

    def move(src, dst):
        copy = pltpu.make_async_copy(src, dst, local.at[len(stays)])
        copy.start()
        stays.append(copy)
        return copy

    barrier = pltpu.get_barrier_semaphore()
    for device in partners:
        pl.semaphore_signal(barrier, inc=1, device_id=device, device_id_type=pl.DeviceIdType.MESH)
    in_pre = move(pre_in.at[0], pre)
    in_down = move(down_in.at[0], down)
    in_up = move(up_in.at[0], up)
    in_moment = move(moment_in.at[0], moment)
    in_second = move(second_in.at[0], second)
    pl.semaphore_wait(barrier, len(partners))

    def piece(s, count=1):
        return pl.ds(s * PIECE, count * PIECE)

    slot_of = {k: at_x(k) * 2 + c for k in (0, -1, 1, 2)}

    def core_group(k, s):
        if k != 2:
            return core_sem.at[abs(k)]
        return core_sem.at[2 if s < 2 else 3 if s < 6 else 4]

    def share(k, s):
        block = inc.at[slot_of[k], piece(s)]
        put(block, block, core, GATHER, core_group(k, s))

    def from_y(s):
        block = inc.at[t, piece(s)]
        landed(block, y_sem.at[s])
        put(block, block, x_up, GATHER, x_sem.at[s])
        put(block, block, x_dn, GATHER, x_sem.at[s])
        share(0, s)

    def from_x(s):
        landed(inc.at[0, piece(0, 2)], x_sem.at[s])
        share(-1, s)
        share(1, s)

    def pass_on(s):
        k, device = (-1, x_up) if s % 2 == 0 else (1, x_dn)
        block = inc.at[slot_of[k], piece(s)]
        put(block, block, device, GATHER, two_sem.at[s // 2])

    def from_two(s):
        landed(inc.at[0, piece(0, 2)], two_sem.at[s // 2])
        share(2, s)
        share(2, s + 1)

    for s in range(PIECES):
        put(handoff.at[0, piece(s)], inc.at[t, piece(s)], across, GATHER, y_sem.at[s])

    GELU = 128

    def gelu(first, last):
        def body(b, carry):
            rows = pl.ds(pl.multiple_of(b * GELU, GELU), GELU)
            a = pre[rows, :].astype(F32)
            cdf = 0.5 * (1.0 + lax.erf(a * (1.0 / math.sqrt(2.0))))
            slope[rows, :] = cdf + a * jnp.exp(-0.5 * a * a) * (1.0 / math.sqrt(2.0 * math.pi))
            hidden_t[:, rows] = (a * cdf).astype(BF16).T
            return carry

        lax.fori_loop(first, last, body, 0)

    lo, hi = pl.ds(0, HALF), pl.ds(HALF, HALF)

    def rows_of(k, h=None):
        if h is None:
            return pl.ds(pl.multiple_of(at_z(k) * 2 * ROWS, 2 * ROWS), 2 * ROWS)
        return pl.ds(pl.multiple_of((at_z(k) * 2 + at_h(h)) * ROWS, ROWS), ROWS)

    def to_owner(xa, n, k, h):
        put(term.at[xa, rows_of(k, h)], fin_got.at[xa, n], owner(k, h), TERMS, fin_sem.at[xa])

    def send_terms(xa):
        sem = agg_sem.at[xa]
        put(term.at[xa, rows_of(4), lo], agg_got.at[xa, 2, :, lo], owner(2, 0), TERMS, sem)
        put(term.at[xa, rows_of(4), hi], agg_got.at[xa, 2, :, hi], owner(-2, 0), TERMS, sem)
        put(term.at[xa, rows_of(3)], agg_got.at[xa, 0], owner(1, 0), TERMS, sem)
        put(term.at[xa, rows_of(-3)], agg_got.at[xa, 1], owner(-1, 0), TERMS, sem)
        for n, (k, h) in enumerate(near):
            if abs(k) == 1:
                to_owner(xa, n, k, h)
        to_owner(xa, 8, 0, 1)

    def terms(k):
        if k != 1:
            landed(inc.at[pl.ds(0, 1 if k == 0 else 2)], core_sem.at[abs(k)])
        xa = at_x(k)
        block = jnp.concatenate([inc[xa * 2], inc[xa * 2 + 1]], axis=1)
        product = jnp.dot(hidden_t[...], block, preferred_element_type=F32)
        term[xa] = (product * (1.0 / math.sqrt(TOKENS))).astype(BF16)
        send_terms(xa)

    def two_terms(first, last):
        landed(inc.at[0, piece(0, 4 if first == 0 else 2)], core_sem.at[3 if first == 0 else 4])
        xa = at_x(2)
        toks = piece(first, last - first)
        block = jnp.concatenate([inc[xa * 2, toks], inc[xa * 2 + 1, toks]], axis=1)
        product = jnp.dot(hidden_t[:, toks], block, preferred_element_type=F32)
        if first == 0:
            so_far[...] = product
            return
        term[xa] = ((so_far[...] + product) * (1.0 / math.sqrt(TOKENS))).astype(BF16)
        send_terms(xa)

    def aggregate(k):
        xa = at_x(k)
        landed(agg_got.at[xa], agg_sem.at[xa])
        for n, step, half in ((0, 2, lo), (1, -2, hi)):
            rows = rows_of(step)
            term[xa, rows] = (term[xa, rows].astype(F32) + agg_got[xa, n].astype(F32)).astype(BF16)
            more = term[xa, rows, half].astype(F32) + agg_got[xa, 2, :, half].astype(F32)
            term[xa, rows, half] = more.astype(BF16)
        for n, (k, h) in enumerate(near):
            if abs(k) == 2:
                to_owner(xa, n, k, h)

    def block_cols(xa):
        return pl.ds(pl.multiple_of(xa * COLS, COLS), COLS)

    def adam(k):
        xa = at_x(k)
        cols = block_cols(xa)
        own = rows_of(0, 0)
        landed(fin_got.at[xa], fin_sem.at[xa])
        gradient = term[xa, own].astype(F32)
        for n in range(9):
            gradient = gradient + fin_got[xa, n].astype(F32)
        m = 0.9 * moment[:, cols] + 0.1 * gradient
        v = 0.95 * second[:, cols] + 0.05 * gradient * gradient
        new_m[:, cols] = m
        new_v[:, cols] = v
        old = down[own, cols].astype(F32)
        fresh[xa, own] = (old - 0.2 * m / (jnp.sqrt(v) + 1e-08)).astype(BF16)
        block = fresh.at[xa, own]
        for k, h in near:
            put(block, block, owner(k, h), NEW, (row_sem if abs(k) == 1 else ring_sem).at[xa])
        put(block, block, owner(0, 1), NEW, row_sem.at[xa])

    def relay(k):
        xa = at_x(k)
        landed(fresh.at[xa, pl.ds(0, 4 * ROWS)], ring_sem.at[xa])
        half = ROWS // 2
        for k, first in ((2, 0), (-2, half)):
            for h in (1, 0):
                start = (at_z(-k) * 2 + at_h(h)) * ROWS
                part_rows = fresh.at[xa, pl.ds(pl.multiple_of(start + first, half), half)]
                put(part_rows, part_rows, owner(k, 0), NEW, row_sem.at[xa])
                block = fresh.at[xa, rows_of(-k, h)]
                put(block, block, owner(k // 2, 0), NEW, row_sem.at[xa])

    def gathered(k):
        xa = at_x(k)
        landed(fresh.at[xa, pl.ds(0, 11 * ROWS)], row_sem.at[xa])
        move(fresh.at[xa], down_out.at[0, :, block_cols(xa)])

    def chunk(i):
        return pl.ds(i * CHUNK, CHUNK)

    def partial(i):
        if i == 0:
            landed(inc.at[0, piece(0, 2)], core_sem.at[2])
        rows = chunk(i)
        block = jnp.concatenate([inc[s, rows] for s in range(2 * X)], axis=1)
        back = lax.dot_general(block, down[...], (((1,), (1,)), ((), ())), preferred_element_type=F32)
        act = (back * (1.0 / math.sqrt(D)) * slope[rows, :]).astype(BF16)
        value = jnp.dot(act, up[...], preferred_element_type=F32) * (1.0 / math.sqrt(FF))
        value = value.astype(BF16)
        for xa in range(X):
            for ca in range(2):
                s = xa * 2 + ca
                part[ca, xa, rows] = value[:, s * 128 : (s + 1) * 128]
        put(part.at[1 - c, :, rows], part_got.at[:, rows], core, GRAD, pair_sem.at[i])

    def summed(i, k):
        xa = at_x(k)
        rows = chunk(i)
        return part[c, xa, rows].astype(F32) + part_got[xa, rows].astype(F32)

    def x_first(i):
        rows = chunk(i)
        landed(part_got.at[:, rows], pair_sem.at[i])
        way, k = (x_up, -1) if i % 2 == 0 else (x_dn, 1)
        one_send[2, rows] = summed(i, 2).astype(BF16)
        put(one_send.at[2, rows], two_got.at[rows], way, GRAD, far_sem.at[i])
        way, side = (x_dn, 1) if i % 2 == 0 else (x_up, 0)
        one_send[side, rows] = summed(i, k).astype(BF16)
        put(one_send.at[side, rows], one_got.at[side, rows], way, GRAD, last_sem.at[i])

    def x_second(i):
        rows = chunk(i)
        way, side, k = (x_up, 0, 1) if i % 2 == 0 else (x_dn, 1, -1)
        landed(two_got.at[rows], far_sem.at[i])
        one_send[side, rows] = (summed(i, k) + two_got[rows].astype(F32)).astype(BF16)
        put(one_send.at[side, rows], one_got.at[side, rows], way, GRAD, last_sem.at[i])

    def x_last(i):
        rows = chunk(i)
        landed(one_got.at[:, rows], last_sem.at[i])
        both = one_got[0, rows].astype(F32) + one_got[1, rows].astype(F32)
        grad[rows] = (summed(i, 0) + both).astype(BF16)

    in_pre.wait()
    gelu(0, 16)
    for s in range(PIECES):
        from_y(s)
        if s >= 3:
            from_x(s - 3)
    for s in range(5):
        pass_on(s)
    from_x(5)
    pass_on(5)
    from_x(6)
    pass_on(6)
    from_x(7)
    pass_on(7)
    terms(0)
    from_two(0)
    terms(-1)
    from_two(2)
    in_down.wait()
    in_up.wait()
    partial(0)
    terms(1)
    from_two(4)
    aggregate(0)
    from_two(6)
    partial(1)
    two_terms(0, 6)
    x_first(0)
    aggregate(-1)
    two_terms(6, 8)
    x_first(1)
    partial(2)
    aggregate(1)
    partial(3)
    x_first(2)
    in_moment.wait()
    in_second.wait()
    adam(0)
    x_first(3)
    partial(4)
    aggregate(2)
    adam(-1)
    x_first(4)
    x_second(0)
    partial(5)
    x_second(1)
    adam(1)
    x_first(5)
    relay(0)
    partial(6)
    x_second(2)
    x_first(6)
    relay(-1)
    adam(2)
    partial(7)
    x_second(3)
    x_first(7)
    relay(1)
    x_second(4)
    x_last(0)
    gathered(0)
    move(new_m, moment_out.at[0])
    move(new_v, second_out.at[0])
    x_second(5)
    relay(2)
    x_last(1)
    gathered(-1)
    x_second(6)
    x_last(2)
    x_last(3)
    gathered(1)
    x_second(7)
    x_last(4)
    x_last(5)
    x_last(6)
    x_last(7)
    move(grad, grad_out.at[0])
    gathered(2)
    left(inc, GATHER)
    left(term.at[:, pl.ds(0, 15 * ROWS)], TERMS)
    left(fresh.at[:, pl.ds(0, 15 * ROWS)], NEW)
    left(inc.at[pl.ds(0, 7)], GRAD)
    for copy in stays[5:]:
        copy.wait()


def place(
    grad, down, moment, second, grad_out, down_out, moment_out, second_out,
    grad_here, down_here, moment_here, second_here, loads, stores,
):
    parts = []
    for a, here, b, rows, n in (
        (down, down_here, down_out, HW, 4),
        (grad, grad_here, grad_out, TOK, 2),
        (moment, moment_here, moment_out, ROWS, 1),
        (second, second_here, second_out, ROWS, 1),
    ):
        for i in range(n):
            at = pl.ds(i * (rows // n), rows // n)
            parts.append((a.at[0, at], here.at[at], b.at[0, at]))
    first = [pltpu.make_async_copy(a, here, loads.at[i]) for i, (a, here, _) in enumerate(parts)]
    then = [pltpu.make_async_copy(here, b, stores.at[i]) for i, (_, here, b) in enumerate(parts)]
    for copy in first:
        copy.start()
    for load, store in zip(first, then, strict=True):
        load.wait()
        store.start()
    for copy in then:
        copy.wait()


def on_device(handoff, hidden_pre, down_weight, up_weight, moment, second):
    anywhere = pl.BlockSpec(memory_space=pl.ANY)
    shapes = (
        jax.ShapeDtypeStruct((1, TOK, 128), BF16),
        jax.ShapeDtypeStruct((1, HW, D), BF16),
        jax.ShapeDtypeStruct((1, ROWS, D), F32),
        jax.ShapeDtypeStruct((1, ROWS, D), F32),
    )
    results = pl.pallas_call(
        kernel,
        out_shape=shapes,
        in_specs=[anywhere] * 6,
        out_specs=(anywhere,) * 4,
        scratch_shapes=[
            pltpu.VMEM((2 * X, TOK, 128), BF16),
            pltpu.VMEM((TOK, HW), BF16),
            pltpu.VMEM((HW, TOK), BF16),
            pltpu.VMEM((TOK, HW), F32),
            pltpu.VMEM((HW, D), BF16),
            pltpu.VMEM((HW, D), BF16),
            pltpu.VMEM((ROWS, D), F32),
            pltpu.VMEM((ROWS, D), F32),
            pltpu.VMEM((2, X, TOK, 128), BF16),
            pltpu.VMEM((X, TOK, 128), BF16),
            pltpu.VMEM((TOK, 128), BF16),
            pltpu.VMEM((3, TOK, 128), BF16),
            pltpu.VMEM((2, TOK, 128), BF16),
            pltpu.VMEM((TOK, 128), BF16),
            pltpu.VMEM((X, HW, COLS), BF16),
            pltpu.VMEM((X, 3, 2 * ROWS, COLS), BF16),
            pltpu.VMEM((X, 9, ROWS, COLS), BF16),
            pltpu.VMEM((HW, COLS), F32),
            pltpu.VMEM((ROWS, D), F32),
            pltpu.VMEM((ROWS, D), F32),
            pltpu.VMEM((X, HW, COLS), BF16),
            pltpu.SemaphoreType.DMA((PIECES,)),
            pltpu.SemaphoreType.DMA((PIECES,)),
            pltpu.SemaphoreType.DMA((PIECES // 2,)),
            pltpu.SemaphoreType.DMA((5,)),
            pltpu.SemaphoreType.DMA((CHUNKS,)),
            pltpu.SemaphoreType.DMA((CHUNKS,)),
            pltpu.SemaphoreType.DMA((CHUNKS,)),
            pltpu.SemaphoreType.DMA((X,)),
            pltpu.SemaphoreType.DMA((X,)),
            pltpu.SemaphoreType.DMA((X,)),
            pltpu.SemaphoreType.DMA((X,)),
            pltpu.SemaphoreType.DMA((4,)),
            pltpu.SemaphoreType.DMA((12,)),
        ],
        compiler_params=pltpu.CompilerParams(
            collective_id=0, has_side_effects=True, vmem_limit_bytes=56 * 1024 * 1024
        ),
        cost_estimate=pl.CostEstimate(flops=6 * TOK * HW * D, bytes_accessed=12 << 20, transcendentals=2 * TOK * HW),
    )(handoff, hidden_pre, down_weight, up_weight, moment, second)
    return pl.pallas_call(
        place,
        out_shape=shapes,
        in_specs=[anywhere] * 4,
        out_specs=(anywhere,) * 4,
        scratch_shapes=[
            pltpu.VMEM((TOK, 128), BF16),
            pltpu.VMEM((HW, D), BF16),
            pltpu.VMEM((ROWS, D), F32),
            pltpu.VMEM((ROWS, D), F32),
            pltpu.SemaphoreType.DMA((8,)),
            pltpu.SemaphoreType.DMA((8,)),
        ],
    )(*results)


def solution(mesh):
    placed = (
        P("pipe", "dp", "tensor"),
        P("pipe", "dp", "tensor"),
        P("pipe", "tensor", None),
        P("pipe", "tensor", None),
        P("pipe", ("tensor", "dp"), None),
        P("pipe", ("tensor", "dp"), None),
    )
    return jax.shard_map(
        on_device,
        mesh=mesh,
        in_specs=placed,
        out_specs=(
            P("pipe", "dp", "tensor"),
            P("pipe", "tensor", None),
            P("pipe", ("tensor", "dp"), None),
            P("pipe", ("tensor", "dp"), None),
        ),
        check_vma=False,
    )
```

```python
import math

import jax
import jax.numpy as jnp
from jax import lax
from jax.experimental import pallas as pl
from jax.experimental.pallas import tpu as pltpu
from jax.sharding import PartitionSpec as P

F32 = jnp.float32
BF16 = jnp.bfloat16

X = 4
Z = 8
D = 1024
HW = 512
TOK = 2048
FF = 4096
TOKENS = 32768
ROWS = 32
SIZES = (128, 128, 256, 256, 256, 256, 256, 256, 128, 128)
PIECES = len(SIZES)
EARLY = 6
CHUNKS = 8
CHUNK = TOK // CHUNKS
COLS = D // X
HALF = COLS // 2


def kernel(
    handoff, pre_in, down_in, up_in, moment_in, second_in,
    grad, fresh, new_m, new_v,
    inc, pre, hidden_t, slope, down, up, moment, second,
    part, part_got, two_got, one_send, one_got,
    term, agg_got, fin_got, so_far,
    y_sem, x_sem, two_sem, core_sem, pair_sem, far_sem, last_sem,
    agg_sem, fin_sem, ring_sem, row_sem, send_sem, local,
):
    p = lax.axis_index("pipe")
    d = lax.axis_index("dp")
    t = lax.axis_index("tensor")
    z, yh = lax.div(d, 2), lax.rem(d, 2)
    x, c = lax.div(t, 2), lax.rem(t, 2)

    def at_x(k):
        return lax.rem(x + (k + X), X)

    def at_z(k):
        return lax.rem(z + (k + Z), Z)

    def at_h(h):
        return 1 - yh if h else yh

    def owner(k, h):
        return (p, at_z(k) * 2 + at_h(h), t)

    across = (1 - p, d, t)
    core = (p, d, x * 2 + (1 - c))
    x_up = (p, d, at_x(1) * 2 + c)
    x_dn = (p, d, at_x(-1) * 2 + c)
    x_up_too = (p, d, at_x(1) * 2 + (1 - c))
    x_dn_too = (p, d, at_x(-1) * 2 + (1 - c))
    near = [(k, h) for k in (2, -2, 1, -1) for h in (1, 0)]
    partners = (across, core, x_up, x_dn, x_up_too, x_dn_too, owner(0, 1)) + tuple(owner(k, h) for k, h in near)

    GATHER, TERMS, NEW, GRAD = range(4)

    def put(src, dst, device, kind, sem):
        pltpu.make_async_remote_copy(
            src_ref=src, dst_ref=dst, send_sem=send_sem.at[kind], recv_sem=sem,
            device_id=device, device_id_type=pl.DeviceIdType.MESH,
        ).start()

    def landed(ref, sem):
        pltpu.make_async_remote_copy(
            src_ref=ref, dst_ref=ref, send_sem=send_sem.at[0], recv_sem=sem,
            device_id=core, device_id_type=pl.DeviceIdType.MESH,
        ).wait_recv()

    def left(ref, kind):
        pltpu.make_async_remote_copy(
            src_ref=ref, dst_ref=ref, send_sem=send_sem.at[kind], recv_sem=row_sem.at[0],
            device_id=core, device_id_type=pl.DeviceIdType.MESH,
        ).wait_send()

    stays = []

    def move(src, dst):
        copy = pltpu.make_async_copy(src, dst, local.at[len(stays)])
        copy.start()
        stays.append(copy)
        return copy

    barrier = pltpu.get_barrier_semaphore()
    for device in partners:
        pl.semaphore_signal(barrier, inc=1, device_id=device, device_id_type=pl.DeviceIdType.MESH)
    in_pre = move(pre_in.at[0], pre)
    in_down = move(down_in.at[0], down)
    in_up = move(up_in.at[0], up)
    in_moment = move(moment_in.at[0], moment)
    in_second = move(second_in.at[0], second)
    pl.semaphore_wait(barrier, len(partners))

    def piece(s, count=1):
        return pl.ds(sum(SIZES[:s]), sum(SIZES[s : s + count]))

    def tokens(n):
        return pl.ds(0, n)

    slot_of = {k: at_x(k) * 2 + c for k in (0, -1, 1, 2)}

    def core_group(k, s):
        if k == 2:
            return 4 + s // 2
        return 2 * abs(k) + (0 if s < EARLY else 1)

    def from_core(group):
        if group >= 4:
            landed(inc.at[0, piece(2 * group - 8, 2)], core_sem.at[group])
        else:
            toks = piece(0, EARLY) if group % 2 == 0 else piece(EARLY, PIECES - EARLY)
            landed(inc.at[pl.ds(0, 1 + group // 2), toks], core_sem.at[group])

    def share(k, s):
        block = inc.at[slot_of[k], piece(s)]
        put(block, block, core, GATHER, core_sem.at[core_group(k, s)])

    def from_y(s):
        block = inc.at[t, piece(s)]
        landed(block, y_sem.at[s])
        put(block, block, x_up, GATHER, x_sem.at[s])
        put(block, block, x_dn, GATHER, x_sem.at[s])
        share(0, s)

    def from_x(s):
        landed(inc.at[0, tokens(2 * SIZES[s])], x_sem.at[s])
        share(-1, s)
        share(1, s)

    def pass_on(s):
        k, device = (-1, x_up) if s % 2 == 0 else (1, x_dn)
        block = inc.at[slot_of[k], piece(s)]
        put(block, block, device, GATHER, two_sem.at[s // 2])
        if s >= PIECES - 2:
            put(block, block, x_up_too if s % 2 == 0 else x_dn_too, GATHER, two_sem.at[s // 2])

    def from_two(s):
        if s == PIECES - 2:
            landed(inc.at[0, tokens(4 * SIZES[s])], two_sem.at[s // 2])
            return
        landed(inc.at[0, tokens(2 * SIZES[s])], two_sem.at[s // 2])
        share(2, s)
        share(2, s + 1)

    for s in range(PIECES):
        put(handoff.at[0, piece(s)], inc.at[t, piece(s)], across, GATHER, y_sem.at[s])

    GELU = 128

    def gelu(first, last):
        def body(b, carry):
            rows = pl.ds(pl.multiple_of(b * GELU, GELU), GELU)
            a = pre[rows, :].astype(F32)
            cdf = 0.5 * (1.0 + lax.erf(a * (1.0 / math.sqrt(2.0))))
            slope[rows, :] = cdf + a * jnp.exp(-0.5 * a * a) * (1.0 / math.sqrt(2.0 * math.pi))
            hidden_t[:, rows] = (a * cdf).astype(BF16).T
            return carry

        lax.fori_loop(first, last, body, 0)

    lo, hi = pl.ds(0, HALF), pl.ds(HALF, HALF)

    def rows_of(k, h=None):
        if h is None:
            return pl.ds(pl.multiple_of(at_z(k) * 2 * ROWS, 2 * ROWS), 2 * ROWS)
        return pl.ds(pl.multiple_of((at_z(k) * 2 + at_h(h)) * ROWS, ROWS), ROWS)

    def to_owner(xa, n, k, h):
        put(term.at[xa, rows_of(k, h)], fin_got.at[xa, n], owner(k, h), TERMS, fin_sem.at[xa])

    def send_terms(xa):
        sem = agg_sem.at[xa]
        put(term.at[xa, rows_of(4), lo], agg_got.at[xa, 2, :, lo], owner(2, 0), TERMS, sem)
        put(term.at[xa, rows_of(4), hi], agg_got.at[xa, 2, :, hi], owner(-2, 0), TERMS, sem)
        put(term.at[xa, rows_of(3)], agg_got.at[xa, 0], owner(1, 0), TERMS, sem)
        put(term.at[xa, rows_of(-3)], agg_got.at[xa, 1], owner(-1, 0), TERMS, sem)
        for n, (k, h) in enumerate(near):
            if abs(k) == 1:
                to_owner(xa, n, k, h)
        to_owner(xa, 8, 0, 1)

    def terms(k, first):
        xa = at_x(k)
        toks = piece(0, EARLY) if first else piece(EARLY, PIECES - EARLY)
        block = jnp.concatenate([inc[xa * 2, toks], inc[xa * 2 + 1, toks]], axis=1)
        product = jnp.dot(hidden_t[:, toks], block, preferred_element_type=F32)
        if first:
            so_far[k + 1] = product
            return
        term[xa] = ((so_far[k + 1] + product) * (1.0 / math.sqrt(TOKENS))).astype(BF16)
        send_terms(xa)

    def aggregate(k):
        xa = at_x(k)
        landed(agg_got.at[xa], agg_sem.at[xa])
        for n, step, half in ((0, 2, lo), (1, -2, hi)):
            rows = rows_of(step)
            term[xa, rows] = (term[xa, rows].astype(F32) + agg_got[xa, n].astype(F32)).astype(BF16)
            more = term[xa, rows, half].astype(F32) + agg_got[xa, 2, :, half].astype(F32)
            term[xa, rows, half] = more.astype(BF16)
        for n, (k, h) in enumerate(near):
            if abs(k) == 2:
                to_owner(xa, n, k, h)

    def block_cols(xa):
        return pl.ds(pl.multiple_of(xa * COLS, COLS), COLS)

    def adam(k):
        xa = at_x(k)
        cols = block_cols(xa)
        own = rows_of(0, 0)
        landed(fin_got.at[xa], fin_sem.at[xa])
        gradient = term[xa, own].astype(F32)
        for n in range(9):
            gradient = gradient + fin_got[xa, n].astype(F32)
        m = 0.9 * moment[:, cols] + 0.1 * gradient
        v = 0.95 * second[:, cols] + 0.05 * gradient * gradient
        new_m[:, cols] = m
        new_v[:, cols] = v
        old = down[own, cols].astype(F32)
        fresh[xa, own] = (old - 0.2 * m / (jnp.sqrt(v) + 1e-08)).astype(BF16)
        block = fresh.at[xa, own]
        for k, h in near:
            put(block, block, owner(k, h), NEW, (row_sem if abs(k) == 1 else ring_sem).at[xa])
        put(block, block, owner(0, 1), NEW, row_sem.at[xa])

    def relay(k):
        xa = at_x(k)
        landed(fresh.at[xa, pl.ds(0, 4 * ROWS)], ring_sem.at[xa])
        half = ROWS // 2
        for k, first in ((2, 0), (-2, half)):
            for h in (1, 0):
                start = (at_z(-k) * 2 + at_h(h)) * ROWS
                part_rows = fresh.at[xa, pl.ds(pl.multiple_of(start + first, half), half)]
                put(part_rows, part_rows, owner(k, 0), NEW, row_sem.at[xa])
                block = fresh.at[xa, rows_of(-k, h)]
                put(block, block, owner(k // 2, 0), NEW, row_sem.at[xa])

    def gathered(k):
        xa = at_x(k)
        landed(fresh.at[xa, pl.ds(0, 11 * ROWS)], row_sem.at[xa])

    def chunk(i):
        return pl.ds(i * CHUNK, CHUNK)

    def partial(i):
        rows = chunk(i)
        block = jnp.concatenate([inc[s, rows] for s in range(2 * X)], axis=1)
        back = lax.dot_general(block, down[...], (((1,), (1,)), ((), ())), preferred_element_type=F32)
        act = (back * (1.0 / math.sqrt(D)) * slope[rows, :]).astype(BF16)
        value = jnp.dot(act, up[...], preferred_element_type=F32) * (1.0 / math.sqrt(FF))
        value = value.astype(BF16)
        for xa in range(X):
            for ca in range(2):
                s = xa * 2 + ca
                part[ca, xa, rows] = value[:, s * 128 : (s + 1) * 128]
        put(part.at[1 - c, :, rows], part_got.at[:, rows], core, GRAD, pair_sem.at[i])

    def summed(i, k):
        xa = at_x(k)
        rows = chunk(i)
        return part[c, xa, rows].astype(F32) + part_got[xa, rows].astype(F32)

    def x_first(i):
        rows = chunk(i)
        landed(part_got.at[:, rows], pair_sem.at[i])
        way, k = (x_up, -1) if i % 2 == 0 else (x_dn, 1)
        one_send[2, rows] = summed(i, 2).astype(BF16)
        put(one_send.at[2, rows], two_got.at[rows], way, GRAD, far_sem.at[i])
        way, side = (x_dn, 1) if i % 2 == 0 else (x_up, 0)
        one_send[side, rows] = summed(i, k).astype(BF16)
        put(one_send.at[side, rows], one_got.at[side, rows], way, GRAD, last_sem.at[i])

    def x_second(i):
        rows = chunk(i)
        way, side, k = (x_up, 0, 1) if i % 2 == 0 else (x_dn, 1, -1)
        landed(two_got.at[rows], far_sem.at[i])
        one_send[side, rows] = (summed(i, k) + two_got[rows].astype(F32)).astype(BF16)
        put(one_send.at[side, rows], one_got.at[side, rows], way, GRAD, last_sem.at[i])

    def x_last(i):
        rows = chunk(i)
        landed(one_got.at[:, rows], last_sem.at[i])
        both = one_got[0, rows].astype(F32) + one_got[1, rows].astype(F32)
        grad[rows] = (summed(i, 0) + both).astype(BF16)

    in_pre.wait()
    gelu(0, 16)
    for s in range(PIECES - 1):
        from_y(s)
        if s >= 3:
            from_x(s - 3)
    from_y(9)
    for s in range(6):
        pass_on(s)
    from_x(6)
    pass_on(6)
    from_core(0)
    terms(0, True)
    from_x(7)
    pass_on(7)
    from_x(8)
    pass_on(8)
    from_core(1)
    terms(0, False)
    from_x(9)
    pass_on(9)
    from_two(0)
    from_core(2)
    terms(-1, True)
    from_two(2)
    terms(1, True)
    from_core(3)
    terms(-1, False)
    from_two(4)
    terms(1, False)
    in_down.wait()
    in_up.wait()
    from_core(4)
    partial(0)
    from_two(6)
    aggregate(0)
    from_core(5)
    partial(1)
    from_core(6)
    terms(2, True)
    from_two(8)
    from_core(7)
    terms(2, False)
    x_first(0)
    aggregate(-1)
    partial(2)
    x_first(1)
    aggregate(1)
    partial(3)
    partial(4)
    x_first(2)
    partial(5)
    x_first(3)
    partial(6)
    aggregate(2)
    x_first(4)
    partial(7)
    x_first(5)
    in_moment.wait()
    in_second.wait()
    adam(0)
    x_second(0)
    x_first(6)
    x_second(1)
    adam(-1)
    x_first(7)
    x_second(2)
    adam(1)
    x_second(3)
    adam(2)
    relay(0)
    x_second(4)
    relay(-1)
    x_last(0)
    x_second(5)
    relay(1)
    x_last(1)
    x_second(6)
    relay(2)
    gathered(0)
    x_last(2)
    x_last(3)
    x_second(7)
    gathered(-1)
    x_last(4)
    x_last(5)
    gathered(1)
    x_last(6)
    x_last(7)
    gathered(2)
    left(inc, GATHER)
    left(term.at[:, pl.ds(0, 15 * ROWS)], TERMS)
    left(fresh.at[:, pl.ds(0, 15 * ROWS)], NEW)
    left(inc.at[pl.ds(0, 7)], GRAD)


def place(grad, fresh, moment, second, grad_out, down_out, moment_out, second_out, sems):
    pairs = [(grad, grad_out.at[0]), (moment, moment_out.at[0]), (second, second_out.at[0])]
    pairs += [(fresh.at[i], down_out.at[0, :, pl.ds(i * COLS, COLS)]) for i in range(X)]
    copies = [pltpu.make_async_copy(a, b, sems.at[i]) for i, (a, b) in enumerate(pairs)]
    for copy in copies:
        copy.start()
    for copy in copies:
        copy.wait()


def on_device(handoff, hidden_pre, down_weight, up_weight, moment, second):
    anywhere = pl.BlockSpec(memory_space=pl.ANY)
    shapes = (
        jax.ShapeDtypeStruct((1, TOK, 128), BF16),
        jax.ShapeDtypeStruct((1, HW, D), BF16),
        jax.ShapeDtypeStruct((1, ROWS, D), F32),
        jax.ShapeDtypeStruct((1, ROWS, D), F32),
    )
    results = pl.pallas_call(
        kernel,
        out_shape=(
            pltpu.VMEM((TOK, 128), BF16),
            pltpu.VMEM((X, HW, COLS), BF16),
            pltpu.VMEM((ROWS, D), F32),
            pltpu.VMEM((ROWS, D), F32),
        ),
        in_specs=[anywhere] * 6,
        out_specs=(pl.BlockSpec(memory_space=pltpu.VMEM),) * 4,
        scratch_shapes=[
            pltpu.VMEM((2 * X, TOK, 128), BF16),
            pltpu.VMEM((TOK, HW), BF16),
            pltpu.VMEM((HW, TOK), BF16),
            pltpu.VMEM((TOK, HW), F32),
            pltpu.VMEM((HW, D), BF16),
            pltpu.VMEM((HW, D), BF16),
            pltpu.VMEM((ROWS, D), F32),
            pltpu.VMEM((ROWS, D), F32),
            pltpu.VMEM((2, X, TOK, 128), BF16),
            pltpu.VMEM((X, TOK, 128), BF16),
            pltpu.VMEM((TOK, 128), BF16),
            pltpu.VMEM((3, TOK, 128), BF16),
            pltpu.VMEM((2, TOK, 128), BF16),
            pltpu.VMEM((X, HW, COLS), BF16),
            pltpu.VMEM((X, 3, 2 * ROWS, COLS), BF16),
            pltpu.VMEM((X, 9, ROWS, COLS), BF16),
            pltpu.VMEM((X, HW, COLS), F32),
            pltpu.SemaphoreType.DMA((PIECES,)),
            pltpu.SemaphoreType.DMA((PIECES,)),
            pltpu.SemaphoreType.DMA((PIECES // 2,)),
            pltpu.SemaphoreType.DMA((8,)),
            pltpu.SemaphoreType.DMA((CHUNKS,)),
            pltpu.SemaphoreType.DMA((CHUNKS,)),
            pltpu.SemaphoreType.DMA((CHUNKS,)),
            pltpu.SemaphoreType.DMA((X,)),
            pltpu.SemaphoreType.DMA((X,)),
            pltpu.SemaphoreType.DMA((X,)),
            pltpu.SemaphoreType.DMA((X,)),
            pltpu.SemaphoreType.DMA((4,)),
            pltpu.SemaphoreType.DMA((5,)),
        ],
        compiler_params=pltpu.CompilerParams(
            collective_id=0, has_side_effects=True, vmem_limit_bytes=56 * 1024 * 1024
        ),
        cost_estimate=pl.CostEstimate(flops=6 * TOK * HW * D, bytes_accessed=12 << 20, transcendentals=2 * TOK * HW),
    )(handoff, hidden_pre, down_weight, up_weight, moment, second)
    return pl.pallas_call(
        place,
        out_shape=shapes,
        in_specs=[pl.BlockSpec(memory_space=pltpu.VMEM)] * 4,
        out_specs=(anywhere,) * 4,
        scratch_shapes=[pltpu.SemaphoreType.DMA((7,))],
    )(*(pltpu.with_memory_space_constraint(r, pltpu.VMEM) for r in results))


def solution(mesh):
    placed = (
        P("pipe", "dp", "tensor"),
        P("pipe", "dp", "tensor"),
        P("pipe", "tensor", None),
        P("pipe", "tensor", None),
        P("pipe", ("tensor", "dp"), None),
        P("pipe", ("tensor", "dp"), None),
    )
    return jax.shard_map(
        on_device,
        mesh=mesh,
        in_specs=placed,
        out_specs=(
            P("pipe", "dp", "tensor"),
            P("pipe", "tensor", None),
            P("pipe", ("tensor", "dp"), None),
            P("pipe", ("tensor", "dp"), None),
        ),
        check_vma=False,
    )
```

```python
import math

import jax
import jax.numpy as jnp
from jax import lax
from jax.experimental import pallas as pl
from jax.experimental.pallas import tpu as pltpu
from jax.sharding import PartitionSpec as P

F32 = jnp.float32
BF16 = jnp.bfloat16

X = 4
Z = 8
D = 1024
HW = 512
TOK = 2048
FF = 4096
TOKENS = 32768
ROWS = 32
SIZES = (128, 128, 256, 256, 256, 256, 256, 256, 128, 128)
PIECES = len(SIZES)
EARLY = 6
CHUNKS = 8
CHUNK = TOK // CHUNKS
COLS = D // X
HALF = COLS // 2


def kernel(
    handoff, pre_in, down_in, up_in, moment_in, second_in,
    grad, fresh, new_m, new_v,
    inc, hand_here, pre, hidden_t, slope, down, up, moment, second,
    part, part_got, two_got, one_send, one_got,
    term, agg_got, fin_got, so_far,
    y_sem, x_sem, two_sem, core_sem, pair_sem, far_sem, last_sem,
    agg_sem, fin_sem, ring_sem, row_sem, send_sem, local,
):
    p = lax.axis_index("pipe")
    d = lax.axis_index("dp")
    t = lax.axis_index("tensor")
    z, yh = lax.div(d, 2), lax.rem(d, 2)
    x, c = lax.div(t, 2), lax.rem(t, 2)

    def at_x(k):
        return lax.rem(x + (k + X), X)

    def at_z(k):
        return lax.rem(z + (k + Z), Z)

    def at_h(h):
        return 1 - yh if h else yh

    def owner(k, h):
        return (p, at_z(k) * 2 + at_h(h), t)

    across = (1 - p, d, t)
    core = (p, d, x * 2 + (1 - c))
    x_up = (p, d, at_x(1) * 2 + c)
    x_dn = (p, d, at_x(-1) * 2 + c)
    x_up_too = (p, d, at_x(1) * 2 + (1 - c))
    x_dn_too = (p, d, at_x(-1) * 2 + (1 - c))
    near = [(k, h) for k in (2, -2, 1, -1) for h in (1, 0)]
    beside = near[4:]
    partners = (across, core, x_up, x_dn, x_up_too, x_dn_too, owner(0, 1)) + tuple(owner(k, h) for k, h in near)

    GATHER, TERMS, NEW, GRAD = range(4)

    def put(src, dst, device, kind, sem):
        pltpu.make_async_remote_copy(
            src_ref=src, dst_ref=dst, send_sem=send_sem.at[kind], recv_sem=sem,
            device_id=device, device_id_type=pl.DeviceIdType.MESH,
        ).start()

    def landed(ref, sem):
        pltpu.make_async_remote_copy(
            src_ref=ref, dst_ref=ref, send_sem=send_sem.at[0], recv_sem=sem,
            device_id=core, device_id_type=pl.DeviceIdType.MESH,
        ).wait_recv()

    def left(ref, kind):
        pltpu.make_async_remote_copy(
            src_ref=ref, dst_ref=ref, send_sem=send_sem.at[kind], recv_sem=row_sem.at[0],
            device_id=core, device_id_type=pl.DeviceIdType.MESH,
        ).wait_send()

    stays = []

    def move(src, dst):
        copy = pltpu.make_async_copy(src, dst, local.at[len(stays)])
        copy.start()
        stays.append(copy)
        return copy

    barrier = pltpu.get_barrier_semaphore()
    for device in partners:
        pl.semaphore_signal(barrier, inc=1, device_id=device, device_id_type=pl.DeviceIdType.MESH)
    in_hand = move(handoff.at[0], hand_here)
    in_pre = move(pre_in.at[0], pre)
    in_hand.wait()
    pl.semaphore_wait(barrier, len(partners))

    def piece(s, count=1):
        return pl.ds(sum(SIZES[:s]), sum(SIZES[s : s + count]))

    def tokens(n):
        return pl.ds(0, n)

    slot_of = {k: at_x(k) * 2 + c for k in (0, -1, 1, 2)}

    def core_group(k, s):
        if k == 2:
            return 4 + s // 2
        return 2 * abs(k) + (0 if s < EARLY else 1)

    def from_core(group):
        if group >= 4:
            landed(inc.at[0, piece(2 * group - 8, 2)], core_sem.at[group])
        else:
            toks = piece(0, EARLY) if group % 2 == 0 else piece(EARLY, PIECES - EARLY)
            landed(inc.at[pl.ds(0, 1 + group // 2), toks], core_sem.at[group])

    def share(k, s):
        block = inc.at[slot_of[k], piece(s)]
        put(block, block, core, GATHER, core_sem.at[core_group(k, s)])

    def from_y(s):
        block = inc.at[t, piece(s)]
        landed(block, y_sem.at[s])
        put(block, block, x_up, GATHER, x_sem.at[s])
        put(block, block, x_dn, GATHER, x_sem.at[s])
        share(0, s)

    def from_x(s):
        landed(inc.at[0, tokens(2 * SIZES[s])], x_sem.at[s])
        share(-1, s)
        share(1, s)

    def pass_on(s):
        k, device = (-1, x_up) if s % 2 == 0 else (1, x_dn)
        block = inc.at[slot_of[k], piece(s)]
        put(block, block, device, GATHER, two_sem.at[s // 2])
        if s >= PIECES - 2:
            put(block, block, x_up_too if s % 2 == 0 else x_dn_too, GATHER, two_sem.at[s // 2])

    def from_two(s):
        if s == PIECES - 2:
            landed(inc.at[0, tokens(4 * SIZES[s])], two_sem.at[s // 2])
            return
        landed(inc.at[0, tokens(2 * SIZES[s])], two_sem.at[s // 2])
        share(2, s)
        share(2, s + 1)

    for s in range(PIECES):
        put(hand_here.at[piece(s)], inc.at[t, piece(s)], across, GATHER, y_sem.at[s])
    in_down = move(down_in.at[0], down)
    in_up = move(up_in.at[0], up)
    in_moment = move(moment_in.at[0], moment)
    in_second = move(second_in.at[0], second)

    GELU = 128

    def gelu(first, last):
        def body(b, carry):
            rows = pl.ds(pl.multiple_of(b * GELU, GELU), GELU)
            a = pre[rows, :].astype(F32)
            cdf = 0.5 * (1.0 + lax.erf(a * (1.0 / math.sqrt(2.0))))
            slope[rows, :] = cdf + a * jnp.exp(-0.5 * a * a) * (1.0 / math.sqrt(2.0 * math.pi))
            hidden_t[:, rows] = (a * cdf).astype(BF16).T
            return carry

        lax.fori_loop(first, last, body, 0)

    lo, hi = pl.ds(0, HALF), pl.ds(HALF, HALF)

    def rows_of(k, h):
        return pl.ds(pl.multiple_of((at_z(k) * 2 + at_h(h)) * ROWS, ROWS), ROWS)

    def send_far(k):
        xa = at_x(k)
        sem = agg_sem.at[xa]
        for h in (1, 0):
            rows = rows_of(4, h)
            put(term.at[xa, rows, lo], agg_got.at[xa, 6 + h, :, lo], owner(2, h), TERMS, sem)
            put(term.at[xa, rows, hi], agg_got.at[xa, 6 + h, :, hi], owner(-2, h), TERMS, sem)
        for n, step in enumerate((1, -1)):
            for h in (1, 0):
                put(term.at[xa, rows_of(3 * step, h)], agg_got.at[xa, 2 * n + h], owner(step, h), TERMS, sem)
            put(term.at[xa, rows_of(2 * step, 1)], agg_got.at[xa, 4 + n], owner(0, 1), TERMS, sem)

    def send_near(k):
        xa = at_x(k)
        for n, (step, h) in enumerate(beside):
            put(term.at[xa, rows_of(step, h)], fin_got.at[xa, n], owner(step, h), TERMS, fin_sem.at[xa])
        put(term.at[xa, rows_of(0, 1)], fin_got.at[xa, 4], owner(0, 1), TERMS, fin_sem.at[xa])

    def terms(k, first):
        xa = at_x(k)
        toks = piece(0, EARLY) if first else piece(EARLY, PIECES - EARLY)
        block = jnp.concatenate([inc[xa * 2, toks], inc[xa * 2 + 1, toks]], axis=1)
        product = jnp.dot(hidden_t[:, toks], block, preferred_element_type=F32)
        if first:
            so_far[k + 1] = product
            return
        term[xa] = ((so_far[k + 1] + product) * (1.0 / math.sqrt(TOKENS))).astype(BF16)
        send_far(k)

    def aggregate(k):
        xa = at_x(k)
        landed(agg_got.at[xa], agg_sem.at[xa])
        for n, step in enumerate((2, -2)):
            rows = rows_of(step, 0)
            mine = term[xa, rows].astype(F32) + agg_got[xa, 4 + n].astype(F32)
            mine = mine + (agg_got[xa, 2 * n].astype(F32) + agg_got[xa, 2 * n + 1].astype(F32))
            side = slice(0, HALF) if n == 0 else slice(HALF, COLS)
            more = agg_got[xa, 6, :, side].astype(F32) + agg_got[xa, 7, :, side].astype(F32)
            whole = [mine[:, :HALF], mine[:, HALF:]]
            whole[n] = whole[n] + more
            term[xa, rows] = jnp.concatenate(whole, axis=1).astype(BF16)
            put(term.at[xa, rows], fin_got.at[xa, 5 + n], owner(step, 0), TERMS, fin_sem.at[xa])

    def block_cols(xa):
        return pl.ds(pl.multiple_of(xa * COLS, COLS), COLS)

    def adam(k):
        xa = at_x(k)
        cols = block_cols(xa)
        own = rows_of(0, 0)
        landed(fin_got.at[xa], fin_sem.at[xa])
        gradient = term[xa, own].astype(F32)
        for n in range(7):
            gradient = gradient + fin_got[xa, n].astype(F32)
        m = 0.9 * moment[:, cols] + 0.1 * gradient
        v = 0.95 * second[:, cols] + 0.05 * gradient * gradient
        new_m[:, cols] = m
        new_v[:, cols] = v
        old = down[own, cols].astype(F32)
        fresh[xa, own] = (old - 0.2 * m / (jnp.sqrt(v) + 1e-08)).astype(BF16)
        block = fresh.at[xa, own]
        for step in (2, -2):
            put(block, block, owner(step, 0), NEW, ring_sem.at[xa])
        for step, h in beside:
            put(block, block, owner(step, h), NEW, row_sem.at[xa])
        put(block, block, owner(0, 1), NEW, row_sem.at[xa])

    def relay(k):
        xa = at_x(k)
        landed(fresh.at[xa, pl.ds(0, 2 * ROWS)], ring_sem.at[xa])
        half = ROWS // 2
        for step, first in ((1, 0), (-1, half)):
            block = fresh.at[xa, rows_of(-2 * step, 0)]
            start = (at_z(-2 * step) * 2 + yh) * ROWS + first
            part_rows = fresh.at[xa, pl.ds(pl.multiple_of(start, half), half)]
            for h in (1, 0):
                put(part_rows, part_rows, owner(2 * step, h), NEW, row_sem.at[xa])
            for h in (1, 0):
                put(block, block, owner(step, h), NEW, row_sem.at[xa])
            put(block, block, owner(0, 1), NEW, row_sem.at[xa])

    def gathered(k):
        xa = at_x(k)
        landed(fresh.at[xa, pl.ds(0, 13 * ROWS)], row_sem.at[xa])

    def chunk(i):
        return pl.ds(i * CHUNK, CHUNK)

    def partial(i):
        rows = chunk(i)
        block = jnp.concatenate([inc[s, rows] for s in range(2 * X)], axis=1)
        back = lax.dot_general(block, down[...], (((1,), (1,)), ((), ())), preferred_element_type=F32)
        act = (back * (1.0 / math.sqrt(D)) * slope[rows, :]).astype(BF16)
        value = jnp.dot(act, up[...], preferred_element_type=F32) * (1.0 / math.sqrt(FF))
        value = value.astype(BF16)
        for xa in range(X):
            for ca in range(2):
                s = xa * 2 + ca
                part[ca, xa, rows] = value[:, s * 128 : (s + 1) * 128]
        put(part.at[1 - c, :, rows], part_got.at[:, rows], core, GRAD, pair_sem.at[i])

    def summed(i, k):
        xa = at_x(k)
        rows = chunk(i)
        return part[c, xa, rows].astype(F32) + part_got[xa, rows].astype(F32)

    def x_first(i):
        rows = chunk(i)
        landed(part_got.at[:, rows], pair_sem.at[i])
        way, k = (x_up, -1) if i % 2 == 0 else (x_dn, 1)
        one_send[2, rows] = summed(i, 2).astype(BF16)
        put(one_send.at[2, rows], two_got.at[rows], way, GRAD, far_sem.at[i])
        way, side = (x_dn, 1) if i % 2 == 0 else (x_up, 0)
        one_send[side, rows] = summed(i, k).astype(BF16)
        put(one_send.at[side, rows], one_got.at[side, rows], way, GRAD, last_sem.at[i])

    def x_second(i):
        rows = chunk(i)
        way, side, k = (x_up, 0, 1) if i % 2 == 0 else (x_dn, 1, -1)
        landed(two_got.at[rows], far_sem.at[i])
        one_send[side, rows] = (summed(i, k) + two_got[rows].astype(F32)).astype(BF16)
        put(one_send.at[side, rows], one_got.at[side, rows], way, GRAD, last_sem.at[i])

    def x_last(i):
        rows = chunk(i)
        landed(one_got.at[:, rows], last_sem.at[i])
        both = one_got[0, rows].astype(F32) + one_got[1, rows].astype(F32)
        grad[rows] = (summed(i, 0) + both).astype(BF16)

    from_y(0)
    in_pre.wait()
    gelu(0, 2)
    from_y(1)
    gelu(2, 6)
    from_y(2)
    gelu(6, 10)
    from_y(3)
    from_x(0)
    gelu(10, 14)
    from_y(4)
    from_x(1)
    gelu(14, 16)
    from_y(5)
    from_x(2)
    from_y(6)
    from_x(3)
    from_y(7)
    from_x(4)
    from_y(8)
    from_x(5)
    from_y(9)
    for s in range(6):
        pass_on(s)
    from_core(0)
    terms(0, True)
    from_x(6)
    pass_on(6)
    from_core(2)
    terms(-1, True)
    from_x(7)
    pass_on(7)
    from_core(1)
    terms(0, False)
    send_near(0)
    from_x(8)
    pass_on(8)
    from_x(9)
    pass_on(9)
    terms(1, True)
    from_core(3)
    terms(-1, False)
    from_two(0)
    from_two(2)
    terms(1, False)
    send_near(-1)
    send_near(1)
    in_down.wait()
    in_up.wait()
    from_core(4)
    from_two(4)
    partial(0)
    from_two(6)
    aggregate(0)
    from_core(5)
    partial(1)
    from_core(6)
    terms(2, True)
    x_first(0)
    from_two(8)
    from_core(7)
    terms(2, False)
    send_near(2)
    x_first(1)
    aggregate(-1)
    partial(2)
    partial(3)
    aggregate(1)
    x_first(2)
    in_moment.wait()
    in_second.wait()
    adam(0)
    partial(4)
    x_first(3)
    x_second(0)
    partial(5)
    x_first(4)
    x_second(1)
    aggregate(2)
    partial(6)
    x_first(5)
    adam(-1)
    adam(1)
    partial(7)
    x_first(6)
    x_second(2)
    x_first(7)
    x_second(3)
    relay(0)
    adam(2)
    relay(-1)
    relay(1)
    x_second(4)
    x_second(5)
    relay(2)
    x_last(0)
    x_last(1)
    x_second(6)
    x_second(7)
    gathered(0)
    x_last(2)
    x_last(3)
    gathered(-1)
    gathered(1)
    x_last(4)
    x_last(5)
    gathered(2)
    x_last(6)
    x_last(7)
    left(inc, GATHER)
    left(term.at[:, pl.ds(0, 15 * ROWS)], TERMS)
    left(fresh.at[:, pl.ds(0, 15 * ROWS)], NEW)
    left(inc.at[pl.ds(0, 7)], GRAD)


def place(grad, fresh, moment, second, grad_out, down_out, moment_out, second_out, sems):
    pairs = [(grad, grad_out.at[0]), (moment, moment_out.at[0]), (second, second_out.at[0])]
    pairs += [(fresh.at[i], down_out.at[0, :, pl.ds(i * COLS, COLS)]) for i in range(X)]
    copies = [pltpu.make_async_copy(a, b, sems.at[i]) for i, (a, b) in enumerate(pairs)]
    for copy in copies:
        copy.start()
    for copy in copies:
        copy.wait()


def on_device(handoff, hidden_pre, down_weight, up_weight, moment, second):
    anywhere = pl.BlockSpec(memory_space=pl.ANY)
    shapes = (
        jax.ShapeDtypeStruct((1, TOK, 128), BF16),
        jax.ShapeDtypeStruct((1, HW, D), BF16),
        jax.ShapeDtypeStruct((1, ROWS, D), F32),
        jax.ShapeDtypeStruct((1, ROWS, D), F32),
    )
    results = pl.pallas_call(
        kernel,
        out_shape=(
            pltpu.VMEM((TOK, 128), BF16),
            pltpu.VMEM((X, HW, COLS), BF16),
            pltpu.VMEM((ROWS, D), F32),
            pltpu.VMEM((ROWS, D), F32),
        ),
        in_specs=[anywhere] * 6,
        out_specs=(pl.BlockSpec(memory_space=pltpu.VMEM),) * 4,
        scratch_shapes=[
            pltpu.VMEM((2 * X, TOK, 128), BF16),
            pltpu.VMEM((TOK, 128), BF16),
            pltpu.VMEM((TOK, HW), BF16),
            pltpu.VMEM((HW, TOK), BF16),
            pltpu.VMEM((TOK, HW), F32),
            pltpu.VMEM((HW, D), BF16),
            pltpu.VMEM((HW, D), BF16),
            pltpu.VMEM((ROWS, D), F32),
            pltpu.VMEM((ROWS, D), F32),
            pltpu.VMEM((2, X, TOK, 128), BF16),
            pltpu.VMEM((X, TOK, 128), BF16),
            pltpu.VMEM((TOK, 128), BF16),
            pltpu.VMEM((3, TOK, 128), BF16),
            pltpu.VMEM((2, TOK, 128), BF16),
            pltpu.VMEM((X, HW, COLS), BF16),
            pltpu.VMEM((X, 8, ROWS, COLS), BF16),
            pltpu.VMEM((X, 7, ROWS, COLS), BF16),
            pltpu.VMEM((X, HW, COLS), F32),
            pltpu.SemaphoreType.DMA((PIECES,)),
            pltpu.SemaphoreType.DMA((PIECES,)),
            pltpu.SemaphoreType.DMA((PIECES // 2,)),
            pltpu.SemaphoreType.DMA((8,)),
            pltpu.SemaphoreType.DMA((CHUNKS,)),
            pltpu.SemaphoreType.DMA((CHUNKS,)),
            pltpu.SemaphoreType.DMA((CHUNKS,)),
            pltpu.SemaphoreType.DMA((X,)),
            pltpu.SemaphoreType.DMA((X,)),
            pltpu.SemaphoreType.DMA((X,)),
            pltpu.SemaphoreType.DMA((X,)),
            pltpu.SemaphoreType.DMA((4,)),
            pltpu.SemaphoreType.DMA((6,)),
        ],
        compiler_params=pltpu.CompilerParams(
            collective_id=0, has_side_effects=True, vmem_limit_bytes=56 * 1024 * 1024
        ),
        cost_estimate=pl.CostEstimate(flops=6 * TOK * HW * D, bytes_accessed=12 << 20, transcendentals=2 * TOK * HW),
    )(handoff, hidden_pre, down_weight, up_weight, moment, second)
    return pl.pallas_call(
        place,
        out_shape=shapes,
        in_specs=[pl.BlockSpec(memory_space=pltpu.VMEM)] * 4,
        out_specs=(anywhere,) * 4,
        scratch_shapes=[pltpu.SemaphoreType.DMA((7,))],
    )(*(pltpu.with_memory_space_constraint(r, pltpu.VMEM) for r in results))


def solution(mesh):
    placed = (
        P("pipe", "dp", "tensor"),
        P("pipe", "dp", "tensor"),
        P("pipe", "tensor", None),
        P("pipe", "tensor", None),
        P("pipe", ("tensor", "dp"), None),
        P("pipe", ("tensor", "dp"), None),
    )
    return jax.shard_map(
        on_device,
        mesh=mesh,
        in_specs=placed,
        out_specs=(
            P("pipe", "dp", "tensor"),
            P("pipe", "tensor", None),
            P("pipe", ("tensor", "dp"), None),
            P("pipe", ("tensor", "dp"), None),
        ),
        check_vma=False,
    )
```

```python
import math

import jax
import jax.numpy as jnp
from jax import lax
from jax.experimental import pallas as pl
from jax.experimental.pallas import tpu as pltpu
from jax.sharding import PartitionSpec as P

F32 = jnp.float32
BF16 = jnp.bfloat16

X = 4
Z = 8
D = 1024
HW = 512
TOK = 2048
FF = 4096
TOKENS = 32768
ROWS = 32
SIZES = (128, 128, 256, 256, 256, 256, 256, 256, 128, 128)
PIECES = len(SIZES)
EARLY = 6
CHUNKS = 8
CHUNK = TOK // CHUNKS
COLS = D // X
HALF = COLS // 2


def kernel(
    handoff, pre_in, down_in, up_in, moment_in, second_in,
    grad, fresh, new_m, new_v,
    inc, hand_here, pre, hidden_t, slope, down, up, moment, second,
    part, part_got, two_got, one_send, one_got,
    term, agg_got, fin_got, so_far,
    y_sem, x_sem, two_sem, core_sem, pair_sem, far_sem, last_sem,
    agg_sem, fin_sem, ring_sem, tail_sem, row_sem, send_sem, local,
):
    p = lax.axis_index("pipe")
    d = lax.axis_index("dp")
    t = lax.axis_index("tensor")
    z, yh = lax.div(d, 2), lax.rem(d, 2)
    x, c = lax.div(t, 2), lax.rem(t, 2)

    def at_x(k):
        return lax.rem(x + (k + X), X)

    def at_z(k):
        return lax.rem(z + (k + Z), Z)

    def at_h(h):
        return 1 - yh if h else yh

    def owner(k, h):
        return (p, at_z(k) * 2 + at_h(h), t)

    across = (1 - p, d, t)
    core = (p, d, x * 2 + (1 - c))
    x_up = (p, d, at_x(1) * 2 + c)
    x_dn = (p, d, at_x(-1) * 2 + c)
    x_up_too = (p, d, at_x(1) * 2 + (1 - c))
    x_dn_too = (p, d, at_x(-1) * 2 + (1 - c))
    near = [(k, h) for k in (2, -2, 1, -1) for h in (1, 0)]
    beside = near[4:]
    partners = (across, core, x_up, x_dn, x_up_too, x_dn_too, owner(0, 1)) + tuple(owner(k, h) for k, h in near)

    GATHER, TERMS, NEW, GRAD = range(4)

    def put(src, dst, device, kind, sem):
        pltpu.make_async_remote_copy(
            src_ref=src, dst_ref=dst, send_sem=send_sem.at[kind], recv_sem=sem,
            device_id=device, device_id_type=pl.DeviceIdType.MESH,
        ).start()

    def landed(ref, sem):
        pltpu.make_async_remote_copy(
            src_ref=ref, dst_ref=ref, send_sem=send_sem.at[0], recv_sem=sem,
            device_id=core, device_id_type=pl.DeviceIdType.MESH,
        ).wait_recv()

    def left(ref, kind):
        pltpu.make_async_remote_copy(
            src_ref=ref, dst_ref=ref, send_sem=send_sem.at[kind], recv_sem=row_sem.at[0],
            device_id=core, device_id_type=pl.DeviceIdType.MESH,
        ).wait_send()

    stays = []

    def move(src, dst):
        copy = pltpu.make_async_copy(src, dst, local.at[len(stays)])
        copy.start()
        stays.append(copy)
        return copy

    barrier = pltpu.get_barrier_semaphore()
    for device in partners:
        pl.semaphore_signal(barrier, inc=1, device_id=device, device_id_type=pl.DeviceIdType.MESH)
    in_hand = move(handoff.at[0], hand_here)
    in_pre = move(pre_in.at[0], pre)
    in_hand.wait()
    pl.semaphore_wait(barrier, len(partners))

    def piece(s, count=1):
        return pl.ds(sum(SIZES[:s]), sum(SIZES[s : s + count]))

    def tokens(n):
        return pl.ds(0, n)

    slot_of = {k: at_x(k) * 2 + c for k in (0, -1, 1, 2)}

    def core_group(k, s):
        if k == 2:
            return 4 + s // 2
        return 2 * abs(k) + (0 if s < EARLY else 1)

    def from_core(group):
        if group >= 4:
            landed(inc.at[0, piece(2 * group - 8, 2)], core_sem.at[group])
        else:
            toks = piece(0, EARLY) if group % 2 == 0 else piece(EARLY, PIECES - EARLY)
            landed(inc.at[pl.ds(0, 1 + group // 2), toks], core_sem.at[group])

    def share(k, s):
        block = inc.at[slot_of[k], piece(s)]
        put(block, block, core, GATHER, core_sem.at[core_group(k, s)])

    def from_y(s):
        block = inc.at[t, piece(s)]
        landed(block, y_sem.at[s])
        put(block, block, x_up, GATHER, x_sem.at[s])
        put(block, block, x_dn, GATHER, x_sem.at[s])
        share(0, s)

    def from_x(s):
        landed(inc.at[0, tokens(2 * SIZES[s])], x_sem.at[s])
        share(-1, s)
        share(1, s)

    def pass_on(s):
        k, device = (-1, x_up) if s % 2 == 0 else (1, x_dn)
        block = inc.at[slot_of[k], piece(s)]
        put(block, block, device, GATHER, two_sem.at[s // 2])
        if s >= PIECES - 2:
            put(block, block, x_up_too if s % 2 == 0 else x_dn_too, GATHER, two_sem.at[s // 2])

    def from_two(s):
        if s == PIECES - 2:
            landed(inc.at[0, tokens(4 * SIZES[s])], two_sem.at[s // 2])
            return
        landed(inc.at[0, tokens(2 * SIZES[s])], two_sem.at[s // 2])
        share(2, s)
        share(2, s + 1)

    def send_y():
        for s in range(PIECES):
            put(hand_here.at[piece(s)], inc.at[t, piece(s)], across, GATHER, y_sem.at[s])


    GELU = 128
    LEAD = 6

    def gelu(first, last):
        def body(b, carry):
            rows = pl.ds(pl.multiple_of(b * GELU, GELU), GELU)
            a = pre[rows, :].astype(F32)
            cdf = 0.5 * (1.0 + lax.erf(a * (1.0 / math.sqrt(2.0))))
            slope[rows, :] = cdf + a * jnp.exp(-0.5 * a * a) * (1.0 / math.sqrt(2.0 * math.pi))
            hidden_t[:, rows] = (a * cdf).astype(BF16).T
            return carry

        lax.fori_loop(first, last, body, 0)

    lo, hi = pl.ds(0, HALF), pl.ds(HALF, HALF)

    def rows_of(k, h):
        return pl.ds(pl.multiple_of((at_z(k) * 2 + at_h(h)) * ROWS, ROWS), ROWS)

    def send_far(k):
        xa = at_x(k)
        sem = agg_sem.at[xa]
        for h in (1, 0):
            rows = rows_of(4, h)
            put(term.at[xa, rows, lo], agg_got.at[xa, 6 + h, :, lo], owner(2, h), TERMS, sem)
            put(term.at[xa, rows, hi], agg_got.at[xa, 6 + h, :, hi], owner(-2, h), TERMS, sem)
        for n, step in enumerate((1, -1)):
            for h in (1, 0):
                put(term.at[xa, rows_of(3 * step, h)], agg_got.at[xa, 2 * n + h], owner(step, h), TERMS, sem)
            put(term.at[xa, rows_of(2 * step, 1)], agg_got.at[xa, 4 + n], owner(0, 1), TERMS, sem)

    def send_near(k):
        xa = at_x(k)
        for n, (step, h) in enumerate(beside):
            put(term.at[xa, rows_of(step, h)], fin_got.at[xa, n], owner(step, h), TERMS, fin_sem.at[xa])
        put(term.at[xa, rows_of(0, 1)], fin_got.at[xa, 4], owner(0, 1), TERMS, fin_sem.at[xa])

    def terms(k, first):
        xa = at_x(k)
        toks = piece(0, EARLY) if first else piece(EARLY, PIECES - EARLY)
        block = jnp.concatenate([inc[xa * 2, toks], inc[xa * 2 + 1, toks]], axis=1)
        product = jnp.dot(hidden_t[:, toks], block, preferred_element_type=F32)
        if first:
            so_far[k + 1] = product
            return
        term[xa] = ((so_far[k + 1] + product) * (1.0 / math.sqrt(TOKENS))).astype(BF16)
        send_far(k)

    def aggregate(k):
        xa = at_x(k)
        landed(agg_got.at[xa], agg_sem.at[xa])
        for n, step in enumerate((2, -2)):
            rows = rows_of(step, 0)
            mine = term[xa, rows].astype(F32) + agg_got[xa, 4 + n].astype(F32)
            mine = mine + (agg_got[xa, 2 * n].astype(F32) + agg_got[xa, 2 * n + 1].astype(F32))
            side = slice(0, HALF) if n == 0 else slice(HALF, COLS)
            more = agg_got[xa, 6, :, side].astype(F32) + agg_got[xa, 7, :, side].astype(F32)
            whole = [mine[:, :HALF], mine[:, HALF:]]
            whole[n] = whole[n] + more
            term[xa, rows] = jnp.concatenate(whole, axis=1).astype(BF16)
            put(term.at[xa, rows], fin_got.at[xa, 5 + n], owner(step, 0), TERMS, fin_sem.at[xa])

    def block_cols(xa):
        return pl.ds(pl.multiple_of(xa * COLS, COLS), COLS)

    def adam(k):
        xa = at_x(k)
        cols = block_cols(xa)
        own = rows_of(0, 0)
        landed(fin_got.at[xa], fin_sem.at[xa])
        gradient = term[xa, own].astype(F32)
        for n in range(7):
            gradient = gradient + fin_got[xa, n].astype(F32)
        m = 0.9 * moment[:, cols] + 0.1 * gradient
        v = 0.95 * second[:, cols] + 0.05 * gradient * gradient
        new_m[:, cols] = m
        new_v[:, cols] = v
        old = down[own, cols].astype(F32)
        fresh[xa, own] = (old - 0.2 * m / (jnp.sqrt(v) + 1e-08)).astype(BF16)
        block = fresh.at[xa, own]
        for step in (2, -2):
            put(block, block, owner(step, 0), NEW, ring_sem.at[xa])
        for step, h in beside:
            put(block, block, owner(step, h), NEW, row_sem.at[xa])
        put(block, block, owner(0, 1), NEW, row_sem.at[xa])

    def pass_rows(xa, h, step, sides):
        half = ROWS // 2
        start = (at_z(-2 * step) * 2 + at_h(h)) * ROWS + (0 if step == 1 else half)
        part_rows = fresh.at[xa, pl.ds(pl.multiple_of(start, half), half)]
        block = fresh.at[xa, rows_of(-2 * step, h)]
        for side in sides:
            put(part_rows, part_rows, owner(2 * step, side), NEW, row_sem.at[xa])
        for side in sides:
            put(block, block, owner(step, side), NEW, row_sem.at[xa])

    def relay(k):
        xa = at_x(k)
        landed(fresh.at[xa, pl.ds(0, 2 * ROWS)], ring_sem.at[xa])
        for step in (1, -1):
            block = fresh.at[xa, rows_of(-2 * step, 0)]
            put(block, block, owner(0, 1), NEW, (row_sem if k == 2 else tail_sem).at[xa])
        for step in (1, -1):
            pass_rows(xa, 0, step, (1, 0) if k == 2 else (0,))

    def cross(k):
        xa = at_x(k)
        landed(fresh.at[xa, pl.ds(0, 2 * ROWS)], tail_sem.at[xa])
        for step in (1, -1):
            pass_rows(xa, 1, step, (0,))

    def gathered(k):
        xa = at_x(k)
        landed(fresh.at[xa, pl.ds(0, (13 if k == 2 else 11) * ROWS)], row_sem.at[xa])

    def chunk(i):
        return pl.ds(i * CHUNK, CHUNK)

    def partial(i):
        rows = chunk(i)
        block = jnp.concatenate([inc[s, rows] for s in range(2 * X)], axis=1)
        back = lax.dot_general(block, down[...], (((1,), (1,)), ((), ())), preferred_element_type=F32)
        act = (back * (1.0 / math.sqrt(D)) * slope[rows, :]).astype(BF16)
        value = jnp.dot(act, up[...], preferred_element_type=F32) * (1.0 / math.sqrt(FF))
        value = value.astype(BF16)
        for xa in range(X):
            for ca in range(2):
                s = xa * 2 + ca
                part[ca, xa, rows] = value[:, s * 128 : (s + 1) * 128]
        put(part.at[1 - c, :, rows], part_got.at[:, rows], core, GRAD, pair_sem.at[i])

    def summed(i, k):
        xa = at_x(k)
        rows = chunk(i)
        return part[c, xa, rows].astype(F32) + part_got[xa, rows].astype(F32)

    def x_first(i):
        rows = chunk(i)
        landed(part_got.at[:, rows], pair_sem.at[i])
        way, k = (x_up, -1) if i % 2 == 0 else (x_dn, 1)
        one_send[2, rows] = summed(i, 2).astype(BF16)
        put(one_send.at[2, rows], two_got.at[rows], way, GRAD, far_sem.at[i])
        way, side = (x_dn, 1) if i % 2 == 0 else (x_up, 0)
        one_send[side, rows] = summed(i, k).astype(BF16)
        put(one_send.at[side, rows], one_got.at[side, rows], way, GRAD, last_sem.at[i])

    def x_second(i):
        rows = chunk(i)
        way, side, k = (x_up, 0, 1) if i % 2 == 0 else (x_dn, 1, -1)
        landed(two_got.at[rows], far_sem.at[i])
        one_send[side, rows] = (summed(i, k) + two_got[rows].astype(F32)).astype(BF16)
        put(one_send.at[side, rows], one_got.at[side, rows], way, GRAD, last_sem.at[i])

    def x_last(i):
        rows = chunk(i)
        landed(one_got.at[:, rows], last_sem.at[i])
        both = one_got[0, rows].astype(F32) + one_got[1, rows].astype(F32)
        grad[rows] = (summed(i, 0) + both).astype(BF16)

    ahead = LEAD * c
    in_pre.wait()
    gelu(0, ahead)
    send_y()
    in_down = move(down_in.at[0], down)
    in_up = move(up_in.at[0], up)
    in_moment = move(moment_in.at[0], moment)
    in_second = move(second_in.at[0], second)
    gelu(ahead, LEAD)
    from_y(0)
    from_y(1)
    gelu(LEAD, 9)
    from_y(2)
    gelu(9, 12)
    from_y(3)
    from_x(0)
    gelu(12, 16)
    from_y(4)
    from_x(1)
    from_y(5)
    from_x(2)
    from_y(6)
    from_x(3)
    from_y(7)
    from_x(4)
    from_y(8)
    from_x(5)
    from_y(9)
    for s in range(6):
        pass_on(s)
    from_core(0)
    terms(0, True)
    from_x(6)
    pass_on(6)
    from_core(2)
    terms(-1, True)
    from_x(7)
    pass_on(7)
    from_core(1)
    terms(0, False)
    send_near(0)
    from_x(8)
    pass_on(8)
    from_x(9)
    pass_on(9)
    terms(1, True)
    from_core(3)
    terms(-1, False)
    from_two(0)
    from_two(2)
    terms(1, False)
    send_near(-1)
    send_near(1)
    in_down.wait()
    in_up.wait()
    from_core(4)
    from_two(4)
    partial(0)
    from_two(6)
    from_core(5)
    pl.when(c == 1)(lambda: partial(1))
    from_core(6)
    terms(2, True)
    aggregate(0)
    x_first(0)
    from_two(8)
    from_core(7)
    terms(2, False)
    send_near(2)
    pl.when(c == 0)(lambda: partial(1))
    aggregate(-1)
    partial(2)
    x_first(1)
    partial(3)
    aggregate(1)
    x_first(2)
    in_moment.wait()
    in_second.wait()
    adam(0)
    partial(4)
    x_first(3)
    aggregate(2)
    x_second(0)
    partial(5)
    x_first(4)
    adam(-1)
    partial(6)
    x_first(5)
    adam(1)
    x_second(1)
    partial(7)
    x_first(6)
    relay(0)
    adam(2)
    x_first(7)
    x_second(2)
    x_second(3)
    relay(-1)
    cross(0)
    relay(1)
    x_second(4)
    relay(2)
    x_second(5)
    cross(-1)
    x_last(0)
    x_last(1)
    cross(1)
    x_second(6)
    x_second(7)
    gathered(0)
    x_last(2)
    x_last(3)
    gathered(-1)
    gathered(1)
    x_last(4)
    x_last(5)
    gathered(2)
    x_last(6)
    x_last(7)
    left(inc, GATHER)
    left(term.at[:, pl.ds(0, 15 * ROWS)], TERMS)
    left(fresh.at[:, pl.ds(0, 15 * ROWS)], NEW)
    left(inc.at[pl.ds(0, 7)], GRAD)


def place(grad, fresh, moment, second, grad_out, down_out, moment_out, second_out, sems):
    pairs = [(grad, grad_out.at[0]), (moment, moment_out.at[0]), (second, second_out.at[0])]
    pairs += [(fresh.at[i], down_out.at[0, :, pl.ds(i * COLS, COLS)]) for i in range(X)]
    copies = [pltpu.make_async_copy(a, b, sems.at[i]) for i, (a, b) in enumerate(pairs)]
    for copy in copies:
        copy.start()
    for copy in copies:
        copy.wait()


def on_device(handoff, hidden_pre, down_weight, up_weight, moment, second):
    anywhere = pl.BlockSpec(memory_space=pl.ANY)
    shapes = (
        jax.ShapeDtypeStruct((1, TOK, 128), BF16),
        jax.ShapeDtypeStruct((1, HW, D), BF16),
        jax.ShapeDtypeStruct((1, ROWS, D), F32),
        jax.ShapeDtypeStruct((1, ROWS, D), F32),
    )
    results = pl.pallas_call(
        kernel,
        out_shape=(
            pltpu.VMEM((TOK, 128), BF16),
            pltpu.VMEM((X, HW, COLS), BF16),
            pltpu.VMEM((ROWS, D), F32),
            pltpu.VMEM((ROWS, D), F32),
        ),
        in_specs=[anywhere] * 6,
        out_specs=(pl.BlockSpec(memory_space=pltpu.VMEM),) * 4,
        scratch_shapes=[
            pltpu.VMEM((2 * X, TOK, 128), BF16),
            pltpu.VMEM((TOK, 128), BF16),
            pltpu.VMEM((TOK, HW), BF16),
            pltpu.VMEM((HW, TOK), BF16),
            pltpu.VMEM((TOK, HW), F32),
            pltpu.VMEM((HW, D), BF16),
            pltpu.VMEM((HW, D), BF16),
            pltpu.VMEM((ROWS, D), F32),
            pltpu.VMEM((ROWS, D), F32),
            pltpu.VMEM((2, X, TOK, 128), BF16),
            pltpu.VMEM((X, TOK, 128), BF16),
            pltpu.VMEM((TOK, 128), BF16),
            pltpu.VMEM((3, TOK, 128), BF16),
            pltpu.VMEM((2, TOK, 128), BF16),
            pltpu.VMEM((X, HW, COLS), BF16),
            pltpu.VMEM((X, 8, ROWS, COLS), BF16),
            pltpu.VMEM((X, 7, ROWS, COLS), BF16),
            pltpu.VMEM((X, HW, COLS), F32),
            pltpu.SemaphoreType.DMA((PIECES,)),
            pltpu.SemaphoreType.DMA((PIECES,)),
            pltpu.SemaphoreType.DMA((PIECES // 2,)),
            pltpu.SemaphoreType.DMA((8,)),
            pltpu.SemaphoreType.DMA((CHUNKS,)),
            pltpu.SemaphoreType.DMA((CHUNKS,)),
            pltpu.SemaphoreType.DMA((CHUNKS,)),
            pltpu.SemaphoreType.DMA((X,)),
            pltpu.SemaphoreType.DMA((X,)),
            pltpu.SemaphoreType.DMA((X,)),
            pltpu.SemaphoreType.DMA((X,)),
            pltpu.SemaphoreType.DMA((X,)),
            pltpu.SemaphoreType.DMA((4,)),
            pltpu.SemaphoreType.DMA((6,)),
        ],
        compiler_params=pltpu.CompilerParams(
            collective_id=0, has_side_effects=True, vmem_limit_bytes=56 * 1024 * 1024
        ),
        cost_estimate=pl.CostEstimate(flops=6 * TOK * HW * D, bytes_accessed=12 << 20, transcendentals=2 * TOK * HW),
    )(handoff, hidden_pre, down_weight, up_weight, moment, second)
    return pl.pallas_call(
        place,
        out_shape=shapes,
        in_specs=[pl.BlockSpec(memory_space=pltpu.VMEM)] * 4,
        out_specs=(anywhere,) * 4,
        scratch_shapes=[pltpu.SemaphoreType.DMA((7,))],
    )(*(pltpu.with_memory_space_constraint(r, pltpu.VMEM) for r in results))


def solution(mesh):
    placed = (
        P("pipe", "dp", "tensor"),
        P("pipe", "dp", "tensor"),
        P("pipe", "tensor", None),
        P("pipe", "tensor", None),
        P("pipe", ("tensor", "dp"), None),
        P("pipe", ("tensor", "dp"), None),
    )
    return jax.shard_map(
        on_device,
        mesh=mesh,
        in_specs=placed,
        out_specs=(
            P("pipe", "dp", "tensor"),
            P("pipe", "tensor", None),
            P("pipe", ("tensor", "dp"), None),
            P("pipe", ("tensor", "dp"), None),
        ),
        check_vma=False,
    )
```

```python
import math

import jax
import jax.numpy as jnp
from jax import lax
from jax.experimental import pallas as pl
from jax.experimental.pallas import tpu as pltpu
from jax.sharding import PartitionSpec as P

F32 = jnp.float32
BF16 = jnp.bfloat16

X = 4
Z = 8
D = 1024
HW = 512
TOK = 2048
FF = 4096
TOKENS = 32768
ROWS = 32
SIZES = (128, 128, 256, 256, 256, 256, 256, 256, 128, 128)
PIECES = len(SIZES)
EARLY = 6
CHUNKS = 8
CHUNK = TOK // CHUNKS
COLS = D // X
HALF = COLS // 2


def kernel(
    handoff, pre_in, down_in, up_in, moment_in, second_in,
    grad, fresh, new_m, new_v,
    inc, hand_here, pre, hidden_t, slope, down, down_t, up, moment, second,
    part, part_got, two_got, one_send, one_got,
    term, agg_got, fin_got, so_far,
    y_sem, x_sem, two_sem, core_sem, pair_sem, far_sem, last_sem,
    agg_sem, fin_sem, ring_sem, tail_sem, row_sem, send_sem, local,
):
    p = lax.axis_index("pipe")
    d = lax.axis_index("dp")
    t = lax.axis_index("tensor")
    z, yh = lax.div(d, 2), lax.rem(d, 2)
    x, c = lax.div(t, 2), lax.rem(t, 2)

    def at_x(k):
        return lax.rem(x + (k + X), X)

    def at_z(k):
        return lax.rem(z + (k + Z), Z)

    def at_h(h):
        return 1 - yh if h else yh

    def owner(k, h):
        return (p, at_z(k) * 2 + at_h(h), t)

    across = (1 - p, d, t)
    core = (p, d, x * 2 + (1 - c))
    x_up = (p, d, at_x(1) * 2 + c)
    x_dn = (p, d, at_x(-1) * 2 + c)
    x_up_too = (p, d, at_x(1) * 2 + (1 - c))
    x_dn_too = (p, d, at_x(-1) * 2 + (1 - c))
    near = [(k, h) for k in (2, -2, 1, -1) for h in (1, 0)]
    beside = near[4:]
    partners = (across, core, x_up, x_dn, x_up_too, x_dn_too, owner(0, 1)) + tuple(owner(k, h) for k, h in near)

    GATHER, TERMS, NEW, GRAD = range(4)

    def put(src, dst, device, kind, sem):
        pltpu.make_async_remote_copy(
            src_ref=src, dst_ref=dst, send_sem=send_sem.at[kind], recv_sem=sem,
            device_id=device, device_id_type=pl.DeviceIdType.MESH,
        ).start()

    def landed(ref, sem):
        pltpu.make_async_remote_copy(
            src_ref=ref, dst_ref=ref, send_sem=send_sem.at[0], recv_sem=sem,
            device_id=core, device_id_type=pl.DeviceIdType.MESH,
        ).wait_recv()

    def left(ref, kind):
        pltpu.make_async_remote_copy(
            src_ref=ref, dst_ref=ref, send_sem=send_sem.at[kind], recv_sem=row_sem.at[0],
            device_id=core, device_id_type=pl.DeviceIdType.MESH,
        ).wait_send()

    stays = []

    def move(src, dst):
        copy = pltpu.make_async_copy(src, dst, local.at[len(stays)])
        copy.start()
        stays.append(copy)
        return copy

    barrier = pltpu.get_barrier_semaphore()
    for device in partners:
        pl.semaphore_signal(barrier, inc=1, device_id=device, device_id_type=pl.DeviceIdType.MESH)
    in_hand = move(handoff.at[0], hand_here)
    in_pre = move(pre_in.at[0], pre)
    in_hand.wait()
    pl.semaphore_wait(barrier, len(partners))

    def piece(s, count=1):
        return pl.ds(sum(SIZES[:s]), sum(SIZES[s : s + count]))

    def tokens(n):
        return pl.ds(0, n)

    slot_of = {k: at_x(k) * 2 + c for k in (0, -1, 1, 2)}

    def core_group(k, s):
        if k == 2:
            return 4 + s // 2
        return 2 * abs(k) + (0 if s < EARLY else 1)

    def from_core(group):
        if group >= 4:
            landed(inc.at[0, piece(2 * group - 8, 2)], core_sem.at[group])
        else:
            toks = piece(0, EARLY) if group % 2 == 0 else piece(EARLY, PIECES - EARLY)
            landed(inc.at[pl.ds(0, 1 + group // 2), toks], core_sem.at[group])

    def share(k, s):
        block = inc.at[slot_of[k], piece(s)]
        put(block, block, core, GATHER, core_sem.at[core_group(k, s)])

    def from_y(s):
        block = inc.at[t, piece(s)]
        landed(block, y_sem.at[s])
        put(block, block, x_up, GATHER, x_sem.at[s])
        put(block, block, x_dn, GATHER, x_sem.at[s])
        share(0, s)

    def from_x(s):
        landed(inc.at[0, tokens(2 * SIZES[s])], x_sem.at[s])
        share(-1, s)
        share(1, s)

    def pass_on(s):
        k, device = (-1, x_up) if s % 2 == 0 else (1, x_dn)
        block = inc.at[slot_of[k], piece(s)]
        put(block, block, device, GATHER, two_sem.at[s // 2])
        if s >= PIECES - 2:
            put(block, block, x_up_too if s % 2 == 0 else x_dn_too, GATHER, two_sem.at[s // 2])

    def from_two(s):
        if s == PIECES - 2:
            landed(inc.at[0, tokens(4 * SIZES[s])], two_sem.at[s // 2])
            return
        landed(inc.at[0, tokens(2 * SIZES[s])], two_sem.at[s // 2])
        share(2, s)
        share(2, s + 1)

    def send_y():
        for s in range(PIECES):
            put(hand_here.at[piece(s)], inc.at[t, piece(s)], across, GATHER, y_sem.at[s])


    GELU = 128
    LEAD = 4

    def gelu(first, last):
        def body(b, carry):
            rows = pl.ds(pl.multiple_of(b * GELU, GELU), GELU)
            a = pre[rows, :].astype(F32)
            cdf = 0.5 * (1.0 + lax.erf(a * (1.0 / math.sqrt(2.0))))
            slope[rows, :] = cdf + a * jnp.exp(-0.5 * a * a) * (1.0 / math.sqrt(2.0 * math.pi))
            hidden_t[:, rows] = (a * cdf).astype(BF16).T
            return carry

        lax.fori_loop(first, last, body, 0)

    lo, hi = pl.ds(0, HALF), pl.ds(HALF, HALF)

    def rows_of(k, h):
        return pl.ds(pl.multiple_of((at_z(k) * 2 + at_h(h)) * ROWS, ROWS), ROWS)

    def send_far(k):
        xa = at_x(k)
        sem = agg_sem.at[xa]
        for h in (1, 0):
            rows = rows_of(4, h)
            put(term.at[xa, rows, lo], agg_got.at[xa, 6 + h, :, lo], owner(2, h), TERMS, sem)
            put(term.at[xa, rows, hi], agg_got.at[xa, 6 + h, :, hi], owner(-2, h), TERMS, sem)
        for n, step in enumerate((1, -1)):
            for h in (1, 0):
                put(term.at[xa, rows_of(3 * step, h)], agg_got.at[xa, 2 * n + h], owner(step, h), TERMS, sem)
            put(term.at[xa, rows_of(2 * step, 1)], agg_got.at[xa, 4 + n], owner(0, 1), TERMS, sem)

    def send_near(k):
        xa = at_x(k)
        for n, (step, h) in enumerate(beside):
            put(term.at[xa, rows_of(step, h)], fin_got.at[xa, n], owner(step, h), TERMS, fin_sem.at[xa])
        put(term.at[xa, rows_of(0, 1)], fin_got.at[xa, 4], owner(0, 1), TERMS, fin_sem.at[xa])

    def terms(k, first):
        xa = at_x(k)
        toks = piece(0, EARLY) if first else piece(EARLY, PIECES - EARLY)
        block = jnp.concatenate([inc[xa * 2, toks], inc[xa * 2 + 1, toks]], axis=1)
        product = jnp.dot(hidden_t[:, toks], block, preferred_element_type=F32)
        if first:
            so_far[k + 1] = product
            return
        term[xa] = ((so_far[k + 1] + product) * (1.0 / math.sqrt(TOKENS))).astype(BF16)
        send_far(k)

    def aggregate(k):
        xa = at_x(k)
        landed(agg_got.at[xa], agg_sem.at[xa])
        for n, step in enumerate((2, -2)):
            rows = rows_of(step, 0)
            mine = term[xa, rows].astype(F32) + agg_got[xa, 4 + n].astype(F32)
            mine = mine + (agg_got[xa, 2 * n].astype(F32) + agg_got[xa, 2 * n + 1].astype(F32))
            side = slice(0, HALF) if n == 0 else slice(HALF, COLS)
            more = agg_got[xa, 6, :, side].astype(F32) + agg_got[xa, 7, :, side].astype(F32)
            whole = [mine[:, :HALF], mine[:, HALF:]]
            whole[n] = whole[n] + more
            term[xa, rows] = jnp.concatenate(whole, axis=1).astype(BF16)
            put(term.at[xa, rows], fin_got.at[xa, 5 + n], owner(step, 0), TERMS, fin_sem.at[xa])

    def block_cols(xa):
        return pl.ds(pl.multiple_of(xa * COLS, COLS), COLS)

    def adam(k):
        xa = at_x(k)
        cols = block_cols(xa)
        own = rows_of(0, 0)
        landed(fin_got.at[xa], fin_sem.at[xa])
        gradient = term[xa, own].astype(F32)
        for n in range(7):
            gradient = gradient + fin_got[xa, n].astype(F32)
        m = 0.9 * moment[:, cols] + 0.1 * gradient
        v = 0.95 * second[:, cols] + 0.05 * gradient * gradient
        new_m[:, cols] = m
        new_v[:, cols] = v
        old = down[own, cols].astype(F32)
        fresh[xa, own] = (old - 0.2 * m / (jnp.sqrt(v) + 1e-08)).astype(BF16)
        block = fresh.at[xa, own]
        for step in (2, -2):
            put(block, block, owner(step, 0), NEW, ring_sem.at[xa])
        for step, h in beside:
            put(block, block, owner(step, h), NEW, row_sem.at[xa])
        put(block, block, owner(0, 1), NEW, row_sem.at[xa])

    def pass_rows(xa, h, step, sides):
        half = ROWS // 2
        start = (at_z(-2 * step) * 2 + at_h(h)) * ROWS + (0 if step == 1 else half)
        part_rows = fresh.at[xa, pl.ds(pl.multiple_of(start, half), half)]
        block = fresh.at[xa, rows_of(-2 * step, h)]
        for side in sides:
            put(part_rows, part_rows, owner(2 * step, side), NEW, row_sem.at[xa])
        for side in sides:
            put(block, block, owner(step, side), NEW, row_sem.at[xa])

    def relay(k):
        xa = at_x(k)
        landed(fresh.at[xa, pl.ds(0, 2 * ROWS)], ring_sem.at[xa])
        for step in (1, -1):
            block = fresh.at[xa, rows_of(-2 * step, 0)]
            put(block, block, owner(0, 1), NEW, (row_sem if k > 0 else tail_sem).at[xa])
        for step in (1, -1):
            pass_rows(xa, 0, step, (1, 0) if k > 0 else (0,))

    def cross(k):
        xa = at_x(k)
        landed(fresh.at[xa, pl.ds(0, 2 * ROWS)], tail_sem.at[xa])
        for step in (1, -1):
            pass_rows(xa, 1, step, (0,))

    def gathered(k):
        xa = at_x(k)
        landed(fresh.at[xa, pl.ds(0, (13 if k > 0 else 11) * ROWS)], row_sem.at[xa])

    def chunk(i):
        return pl.ds(i * CHUNK, CHUNK)

    def turn(n):
        rows = pl.ds(n * 128, 128)
        down_t[:, rows] = down[rows, :].T

    def partial(i):
        rows = chunk(i)
        block = jnp.concatenate([inc[s, rows] for s in range(2 * X)], axis=1)
        back = jnp.dot(block, down_t[...], preferred_element_type=F32)
        act = (back * (1.0 / math.sqrt(D)) * slope[rows, :]).astype(BF16)
        value = jnp.dot(act, up[...], preferred_element_type=F32) * (1.0 / math.sqrt(FF))
        value = value.astype(BF16)
        for xa in range(X):
            for ca in range(2):
                s = xa * 2 + ca
                part[ca, xa, rows] = value[:, s * 128 : (s + 1) * 128]
        put(part.at[1 - c, :, rows], part_got.at[:, rows], core, GRAD, pair_sem.at[i])

    def summed(i, k):
        xa = at_x(k)
        rows = chunk(i)
        return part[c, xa, rows].astype(F32) + part_got[xa, rows].astype(F32)

    def x_first(i):
        rows = chunk(i)
        landed(part_got.at[:, rows], pair_sem.at[i])
        way, k = (x_up, -1) if i % 2 == 0 else (x_dn, 1)
        one_send[2, rows] = summed(i, 2).astype(BF16)
        put(one_send.at[2, rows], two_got.at[rows], way, GRAD, far_sem.at[i])
        way, side = (x_dn, 1) if i % 2 == 0 else (x_up, 0)
        one_send[side, rows] = summed(i, k).astype(BF16)
        put(one_send.at[side, rows], one_got.at[side, rows], way, GRAD, last_sem.at[i])

    def x_second(i):
        rows = chunk(i)
        way, side, k = (x_up, 0, 1) if i % 2 == 0 else (x_dn, 1, -1)
        landed(two_got.at[rows], far_sem.at[i])
        one_send[side, rows] = (summed(i, k) + two_got[rows].astype(F32)).astype(BF16)
        put(one_send.at[side, rows], one_got.at[side, rows], way, GRAD, last_sem.at[i])

    def x_last(i):
        rows = chunk(i)
        landed(one_got.at[:, rows], last_sem.at[i])
        both = one_got[0, rows].astype(F32) + one_got[1, rows].astype(F32)
        grad[rows] = (summed(i, 0) + both).astype(BF16)

    ahead = LEAD * c
    in_pre.wait()
    gelu(0, ahead)
    send_y()
    in_down = move(down_in.at[0], down)
    in_up = move(up_in.at[0], up)
    in_moment = move(moment_in.at[0], moment)
    in_second = move(second_in.at[0], second)
    gelu(ahead, LEAD)
    from_y(0)
    from_y(1)
    gelu(LEAD, 9)
    from_y(2)
    gelu(9, 12)
    from_y(3)
    from_x(0)
    gelu(12, 16)
    from_y(4)
    from_x(1)
    in_down.wait()
    turn(0)
    from_y(5)
    from_x(2)
    turn(1)
    from_y(6)
    from_x(3)
    turn(2)
    from_y(7)
    from_x(4)
    turn(3)
    from_y(8)
    from_x(5)
    from_y(9)
    pass_on(0)
    pass_on(1)
    pass_on(2)
    pass_on(3)
    pass_on(4)
    pass_on(5)
    from_core(0)
    terms(0, True)
    from_x(6)
    pass_on(6)
    from_core(2)
    terms(-1, True)
    from_x(7)
    pass_on(7)
    from_core(1)
    terms(0, False)
    send_near(0)
    from_x(8)
    pass_on(8)
    from_x(9)
    pass_on(9)
    terms(1, True)
    from_core(3)
    terms(-1, False)
    from_two(0)
    from_two(2)
    terms(1, False)
    send_near(-1)
    send_near(1)
    in_up.wait()
    from_core(4)
    from_two(4)
    partial(0)
    from_two(6)
    from_core(5)
    pl.when(c == 1)(lambda: partial(1))
    from_core(6)
    terms(2, True)
    aggregate(0)
    x_first(0)
    from_two(8)
    from_core(7)
    terms(2, False)
    send_near(2)
    pl.when(c == 0)(lambda: partial(1))
    aggregate(-1)
    partial(2)
    x_first(1)
    partial(3)
    aggregate(1)
    x_first(2)
    in_moment.wait()
    in_second.wait()
    adam(0)
    partial(4)
    x_first(3)
    partial(5)
    x_first(4)
    adam(-1)
    aggregate(2)
    x_second(0)
    partial(6)
    x_first(5)
    x_second(1)
    adam(1)
    partial(7)
    x_first(6)
    relay(0)
    x_first(7)
    adam(2)
    x_second(2)
    x_second(3)
    relay(-1)
    relay(1)
    x_second(4)
    cross(0)
    relay(2)
    x_second(5)
    cross(-1)
    x_last(0)
    x_last(1)
    x_second(6)
    x_second(7)
    gathered(0)
    x_last(2)
    x_last(3)
    gathered(-1)
    x_last(4)
    gathered(1)
    x_last(5)
    gathered(2)
    x_last(6)
    x_last(7)
    left(inc, GATHER)
    left(term.at[:, pl.ds(0, 15 * ROWS)], TERMS)
    left(fresh.at[:, pl.ds(0, 15 * ROWS)], NEW)
    left(inc.at[pl.ds(0, 7)], GRAD)


def place(grad, fresh, moment, second, grad_out, down_out, moment_out, second_out, sems):
    pairs = [(grad, grad_out.at[0]), (moment, moment_out.at[0]), (second, second_out.at[0])]
    pairs += [(fresh.at[i], down_out.at[0, :, pl.ds(i * COLS, COLS)]) for i in range(X)]
    copies = [pltpu.make_async_copy(a, b, sems.at[i]) for i, (a, b) in enumerate(pairs)]
    for copy in copies:
        copy.start()
    for copy in copies:
        copy.wait()


def on_device(handoff, hidden_pre, down_weight, up_weight, moment, second):
    anywhere = pl.BlockSpec(memory_space=pl.ANY)
    shapes = (
        jax.ShapeDtypeStruct((1, TOK, 128), BF16),
        jax.ShapeDtypeStruct((1, HW, D), BF16),
        jax.ShapeDtypeStruct((1, ROWS, D), F32),
        jax.ShapeDtypeStruct((1, ROWS, D), F32),
    )
    results = pl.pallas_call(
        kernel,
        out_shape=(
            pltpu.VMEM((TOK, 128), BF16),
            pltpu.VMEM((X, HW, COLS), BF16),
            pltpu.VMEM((ROWS, D), F32),
            pltpu.VMEM((ROWS, D), F32),
        ),
        in_specs=[anywhere] * 6,
        out_specs=(pl.BlockSpec(memory_space=pltpu.VMEM),) * 4,
        scratch_shapes=[
            pltpu.VMEM((2 * X, TOK, 128), BF16),
            pltpu.VMEM((TOK, 128), BF16),
            pltpu.VMEM((TOK, HW), BF16),
            pltpu.VMEM((HW, TOK), BF16),
            pltpu.VMEM((TOK, HW), F32),
            pltpu.VMEM((HW, D), BF16),
            pltpu.VMEM((D, HW), BF16),
            pltpu.VMEM((HW, D), BF16),
            pltpu.VMEM((ROWS, D), F32),
            pltpu.VMEM((ROWS, D), F32),
            pltpu.VMEM((2, X, TOK, 128), BF16),
            pltpu.VMEM((X, TOK, 128), BF16),
            pltpu.VMEM((TOK, 128), BF16),
            pltpu.VMEM((3, TOK, 128), BF16),
            pltpu.VMEM((2, TOK, 128), BF16),
            pltpu.VMEM((X, HW, COLS), BF16),
            pltpu.VMEM((X, 8, ROWS, COLS), BF16),
            pltpu.VMEM((X, 7, ROWS, COLS), BF16),
            pltpu.VMEM((X, HW, COLS), F32),
            pltpu.SemaphoreType.DMA((PIECES,)),
            pltpu.SemaphoreType.DMA((PIECES,)),
            pltpu.SemaphoreType.DMA((PIECES // 2,)),
            pltpu.SemaphoreType.DMA((8,)),
            pltpu.SemaphoreType.DMA((CHUNKS,)),
            pltpu.SemaphoreType.DMA((CHUNKS,)),
            pltpu.SemaphoreType.DMA((CHUNKS,)),
            pltpu.SemaphoreType.DMA((X,)),
            pltpu.SemaphoreType.DMA((X,)),
            pltpu.SemaphoreType.DMA((X,)),
            pltpu.SemaphoreType.DMA((X,)),
            pltpu.SemaphoreType.DMA((X,)),
            pltpu.SemaphoreType.DMA((4,)),
            pltpu.SemaphoreType.DMA((6,)),
        ],
        compiler_params=pltpu.CompilerParams(
            collective_id=0, has_side_effects=True, vmem_limit_bytes=56 * 1024 * 1024
        ),
        cost_estimate=pl.CostEstimate(flops=6 * TOK * HW * D, bytes_accessed=12 << 20, transcendentals=2 * TOK * HW),
    )(handoff, hidden_pre, down_weight, up_weight, moment, second)
    return pl.pallas_call(
        place,
        out_shape=shapes,
        in_specs=[pl.BlockSpec(memory_space=pltpu.VMEM)] * 4,
        out_specs=(anywhere,) * 4,
        scratch_shapes=[pltpu.SemaphoreType.DMA((7,))],
    )(*(pltpu.with_memory_space_constraint(r, pltpu.VMEM) for r in results))


def solution(mesh):
    placed = (
        P("pipe", "dp", "tensor"),
        P("pipe", "dp", "tensor"),
        P("pipe", "tensor", None),
        P("pipe", "tensor", None),
        P("pipe", ("tensor", "dp"), None),
        P("pipe", ("tensor", "dp"), None),
    )
    return jax.shard_map(
        on_device,
        mesh=mesh,
        in_specs=placed,
        out_specs=(
            P("pipe", "dp", "tensor"),
            P("pipe", "tensor", None),
            P("pipe", ("tensor", "dp"), None),
            P("pipe", ("tensor", "dp"), None),
        ),
        check_vma=False,
    )
```
